256 devices in a mesh: clip: 8 (over y_hi, x), seq: 32 (over z, y_lo, core).
Axes of the slice: x: 4, y: 4 (y_hi: 2, y_lo: 2; y = y_hi * 2 + y_lo), z: 8, core: 2. Of those that a mesh axis runs over, the one named last changes fastest.
Arguments:
- latent: float32 [8, 64, 8192], P('clip', None, 'seq'), may hold values from -6 to 6
- sample_noise: float32 [8, 64, 8192], P('clip', None, 'seq'), may hold values from -6 to 6
- vel_cond: bfloat16 [8, 64, 8192], P('clip', None, 'seq'), may hold values from -6 to 6
- vel_uncond: bfloat16 [8, 64, 8192], P('clip', None, 'seq'), may hold values from -6 to 6
- step_index: int32 [1], replicated, may hold values from 0 to 15
- embed_w: bfloat16 [64, 3072], replicated, may hold values from -0.75 to 0.75
- gate_scale: float32 [8, 3072], P('clip'), may hold values from 0.5 to 1.5
- attn_vals: bfloat16 [8, 8192, 1536], P('clip', 'seq'), may hold values from -6 to 6
- out_w: bfloat16 [1536, 3072], P(None, 'clip'), may hold values from -0.15625 to 0.15625
- cotangent: bfloat16 [8, 8192, 3072], P('clip', 'seq'), may hold values from -6 to 6
- rewards: float32 [8], P('clip'), may hold values from 0 to 2
Outputs:
- block_out: bfloat16 [8, 8192, 3072], P('clip', 'seq')
- grad_attn: bfloat16 [8, 8192, 1536], P('clip', 'seq')
- grad_out_w: float32 [1536, 3072], P('seq', 'clip')
- grad_embed_w: float32 [8, 64, 3072], P('clip')
The draws below stay inside these ranges and needn't reach their ends.
Inputs may be any that keep to these rules, and one draw needn't show every extreme that they name: `step_index`: index of the step among the 16 steps of the roster.
All inputs are finite; a program needn't handle non-finite values.
Results may differ from the reference program's by a relative error of at most 0.017.
Values may be sent and summed in bfloat16 or wider, within the bound.
A program may use at most 128 MiB of HBM per device.

```python
import jax
import jax.numpy as jnp

D = 3072
HEAD_DIM = 128
CH = 64
HEADS = 12
NSTEPS = 16
L = 8192
CLIPS = 8


def strengthened(values, key, source, target, shards_of, factor):
    owner, partner = [(jnp.arange(values.shape[position]) // (values.shape[position] // shards_of)).reshape([-1 if axis == position else 1 for axis in range(values.ndim)]) for position in (source, target)]
    chosen = jax.random.permutation(key, shards_of)[partner]
    strong = (owner == chosen) | (owner == (partner + shards_of // 2) % shards_of)
    return jnp.where(strong, factor * values, values)


def steps_of(own_key, dims, cuts, low, high):
    loudness = 1.0
    for dim, shards_of in cuts:
        draws = jax.random.uniform(jax.random.fold_in(jax.random.fold_in(own_key, 6), dim), (shards_of,), jnp.float32, low / len(cuts), high / len(cuts))
        loudness = loudness * jnp.repeat(jnp.exp(draws), dims[dim] // shards_of).reshape((-1,) + (1,) * (len(dims) - 1 - dim))
    return loudness


def noise(stream_key, extent, deviation, reach, split=(), dtype=jnp.bfloat16):
    values = deviation * jax.random.normal(stream_key, extent, jnp.float32)
    if split:
        values = values * steps_of(stream_key, extent, split, -0.22, 0.18)
    return jnp.clip(values, -reach, reach).astype(dtype)


def bell_draw_with(rng, extent, scale, most, pieces, heavy, kind=jnp.bfloat16):
    result = scale * jax.random.normal(rng, extent, jnp.float32)
    if pieces:
        result = result * steps_of(rng, extent, pieces, -0.22, 0.18)
    return jnp.clip(strengthened(result, jax.random.fold_in(rng, 3), *heavy), -most, most).astype(kind)


def setup_inputs(seed: int = 0) -> dict:
    arg_keys = jax.random.split(jax.random.key(seed), 12)
    return {
        "latent": noise(arg_keys[0], (CLIPS, CH, L), 1.0, 6.0, ((0, 8), (2, 32)), jnp.float32),
        "sample_noise": noise(arg_keys[1], (CLIPS, CH, L), 1.0, 6.0, ((0, 8), (2, 32)), jnp.float32),
        "vel_cond": noise(arg_keys[2], (CLIPS, CH, L), 1.0, 6.0, ((0, 8), (2, 32))),
        "vel_uncond": noise(arg_keys[3], (CLIPS, CH, L), 1.0, 6.0, ((0, 8), (2, 32))),
        "step_index": jax.random.randint(arg_keys[4], (1,), 0, NSTEPS).astype(jnp.int32),
        "embed_w": noise(arg_keys[5], (CH, D), CH ** -0.5, 0.75),
        "gate_scale": jnp.clip(0.5 + 1.0 * jax.random.uniform(arg_keys[6], (CLIPS, D), jnp.float32) ** steps_of(arg_keys[6], (CLIPS, D), ((0, 8),), -0.2, 0.2), 0.5, 1.5),
        "attn_vals": noise(arg_keys[7], (CLIPS, L, HEADS * HEAD_DIM), 1.0, 6.0, ((0, 8), (1, 32))),
        "out_w": noise(arg_keys[8], (HEADS * HEAD_DIM, D), (HEADS * HEAD_DIM) ** -0.5, 0.15625, ((1, 8),)),
        "cotangent": bell_draw_with(arg_keys[9], (CLIPS, L, D), 1.0, 6.0, ((0, 8), (1, 32)), (1, 2, 32, 2.75)),
        "rewards": jnp.clip(2.0 * jax.random.uniform(arg_keys[10], (CLIPS,), jnp.float32) ** steps_of(arg_keys[10], (CLIPS,), ((0, 8),), -0.2, 0.2), 0.0, 2.0),
    }


SHIFT_FACTOR = 7.0
GUIDANCE = 6.0
NOISE_LEVEL = 0.3

def sigma_level(index):
    tval = 1.0 - index.astype(jnp.float32) / NSTEPS
    return SHIFT_FACTOR * tval / (1.0 + (SHIFT_FACTOR - 1.0) * tval)

def reference(latent, sample_noise, vel_cond, vel_uncond, step_index, embed_w, gate_scale, attn_vals, out_w, cotangent, rewards):
    sig_now = sigma_level(step_index[0])
    sig_next = sigma_level(step_index[0] + 1)
    uncond = vel_uncond.astype(jnp.float32)
    guided = uncond + GUIDANCE * (vel_cond.astype(jnp.float32) - uncond)
    spread = NOISE_LEVEL * jnp.sqrt(sig_now - sig_next)
    sampled = (latent + (sig_next - sig_now) * guided + spread * sample_noise).astype(jnp.bfloat16)
    embedded = jnp.einsum('ncl,cd->nld', sampled.astype(jnp.float32), embed_w.astype(jnp.float32))
    projected = jnp.einsum('nlh,hd->nld', attn_vals.astype(jnp.float32), out_w.astype(jnp.float32))
    block_out = (embedded + gate_scale[:, None, :] * projected).astype(jnp.bfloat16)
    advantage = rewards - jnp.sum(rewards) / CLIPS
    scaled = (cotangent.astype(jnp.float32) * advantage[:, None, None]).astype(jnp.bfloat16)
    branch = (scaled.astype(jnp.float32) * gate_scale[:, None, :]).astype(jnp.bfloat16)
    grad_attn = jnp.einsum('nld,hd->nlh', branch.astype(jnp.float32), out_w.astype(jnp.float32)).astype(jnp.bfloat16)
    grad_out_w = jnp.einsum('nlh,nld->hd', attn_vals.astype(jnp.float32), branch.astype(jnp.float32))
    grad_embed_w = jnp.einsum('ncl,nld->ncd', sampled.astype(jnp.float32), scaled.astype(jnp.float32))
    return (block_out, grad_attn, grad_out_w, grad_embed_w)
```

```python
import jax
import jax.numpy as jnp
from jax import lax
from jax.experimental import pallas as pl
from jax.experimental.pallas import tpu as pltpu
from jax.sharding import PartitionSpec as P

NSTEPS = 16
SHIFT_FACTOR = 7.0
GUIDANCE = 6.0
NOISE_LEVEL = 0.3

D = 3072
H = 1536
CH = 64
TOK = 256
NX, NZ = 4, 8
CLIPS = 8
SL = D // CLIPS
HALF = H // 2
ROWS = 48
ZROWS = 2 * ROWS
NC = 4
CC = D // NC
TILE = 256
MESH = pl.DeviceIdType.MESH
F32, BF16 = jnp.float32, jnp.bfloat16


def sigma_level(index):
    tval = 1.0 - index.astype(F32) / NSTEPS
    return SHIFT_FACTOR * tval / (1.0 + (SHIFT_FACTOR - 1.0) * tval)


def dev(x, h, lo, z, core):
    return (h * NX + x, z * 4 + lo * 2 + core)


def kernel(
    step_ref, rew_ref, lat_ref, noi_ref, vc_ref, vu_ref, ew_ref, gate_ref, vals_ref, w_ref, cot_ref,
    bo_ref, ga_ref, gw_ref, ge_ref,
    vals_v, cot2, a2, vts, wf, gs, es, zls, zlr, zss, zsr, fs, fr, e1s, e1r, e2s, e2r, ef,
    rsb, rrb, samp_t, branch, gadv, advb, ga_acc,
    loc, r_s, r_r, cot_s, cot_r, a2_s, a2_r, wx_s, wy_s, wc_s, w_r, wc_r,
    zl_s, zl_r, zs_s, zs_r, f_s, f_r, e1_s, e1_r, e2_s, e2_r, e3_s, e3_r, e4_s, e4_r,
):
    clip = lax.axis_index("clip")
    seq = lax.axis_index("seq")
    h, x = lax.div(clip, NX), lax.rem(clip, NX)
    z, lo, core = lax.div(seq, 4), lax.rem(lax.div(seq, 2), 2), lax.rem(seq, 2)
    oc, olo, oh = 1 - core, 1 - lo, 1 - h
    sgn = 1 - 2 * core

    def xr(n):
        return lax.rem(x + n + NX, NX)

    def zr(n):
        return lax.rem(z + n + NZ, NZ)

    def rcopy(src, dst, ss, rs, to):
        return pltpu.make_async_remote_copy(
            src_ref=src, dst_ref=dst, send_sem=ss, recv_sem=rs, device_id=to, device_id_type=MESH
        )

    ld_vals = pltpu.make_async_copy(vals_ref, vals_v, loc.at[0])
    ld_cot = pltpu.make_async_copy(cot_ref, cot2.at[pl.ds(0, TOK)], loc.at[1])
    ld_w0 = pltpu.make_async_copy(w_ref.at[pl.ds(0, HALF)], wf.at[clip, 0], loc.at[2])
    ld_w1 = pltpu.make_async_copy(w_ref.at[pl.ds(HALF, HALF)], wf.at[clip, 1], loc.at[3])
    ld_vals.start()
    ld_cot.start()
    ld_w0.start()
    ld_w1.start()

    bar = pltpu.get_barrier_semaphore()
    me16 = clip * 2 + lo
    partners = []
    for r in range(1, 16):
        o = lax.rem(me16 + r, 16)
        oclip, olo_ = lax.div(o, 2), lax.rem(o, 2)
        partners.append((oclip, z * 4 + olo_ * 2 + core))
    for r in range(1, NZ):
        partners.append(dev(x, h, lo, zr(r), core))
    partners.append(dev(x, h, lo, z, oc))
    partners.append(dev(x, h, olo, z, oc))
    for p in partners:
        pl.semaphore_signal(bar, inc=1, device_id=p, device_id_type=MESH)

    rsb[...] = jnp.full((8, 128), rew_ref[0], F32)
    rrb[clip] = jnp.full((8, 128), rew_ref[0], F32)
    idx = jnp.full((1, TOK), step_ref[0], jnp.int32)
    sig_now = sigma_level(idx)
    sig_next = sigma_level(idx + 1)
    uncond = vu_ref[...].astype(F32)
    guided = uncond + GUIDANCE * (vc_ref[...].astype(F32) - uncond)
    spread = NOISE_LEVEL * jnp.sqrt(sig_now - sig_next)
    sampled = lat_ref[...] + (sig_next - sig_now) * guided + spread * noi_ref[...]
    samp_t[...] = sampled.T.astype(BF16)
    samp_b = sampled.astype(BF16)
    vts[0, pl.ds(HALF, 32), :] = samp_b[0:32]
    vts[1, pl.ds(HALF, 32), :] = samp_b[32:64]

    pl.semaphore_wait(bar, len(partners))

    rsends = []
    for r in range(1, CLIPS):
        c = lax.rem(clip + r, CLIPS)
        cp = rcopy(rsb, rrb.at[clip], r_s.at[r - 1], r_r.at[clip], (c, seq))
        cp.start()
        rsends.append(cp)
    core_dev = dev(x, h, lo, z, oc)
    cp_cot = rcopy(cot_ref, cot2.at[pl.ds(TOK, TOK)], cot_s, cot_r, core_dev)
    cp_cot.start()

    role_c = core == olo
    role_r = core == lo
    side = dev(x, h, olo, z, core)
    cross = dev(x, oh, olo, z, core)
    own_half = w_ref.at[pl.ds(pl.multiple_of(core * HALF, HALF), HALF)]

    def w_own(ss, to):
        return rcopy(own_half, wf.at[clip, core], ss, w_r.at[clip], to)

    def w_fwd(slot, ss, to):
        return rcopy(wf.at[slot, core], wf.at[slot, core], ss, w_r.at[slot], to)

    xp = dev(xr(1), h, lo, z, core)
    xm = dev(xr(-1), h, lo, z, core)
    w_own(wx_s.at[0], xp).start()
    w_own(wx_s.at[1], xm).start()

    @pl.when(role_c)
    def _():
        w_own(wy_s.at[0], cross).start()

    def a_slot(i):
        return h * NX + xr(i)

    def b_slot(i):
        return oh * NX + xr(i)

    def w_core(slot):
        return rcopy(wf.at[slot, core], wf.at[slot, core], wc_s.at[slot], wc_r.at[slot], core_dev)

    def w_core_other(slot):
        return rcopy(wf.at[slot, oc], wf.at[slot, oc], wc_s.at[slot], wc_r.at[slot], core_dev)

    def got(slot):
        w_fwd(slot, wx_s.at[0], xp).wait_recv()
        w_core(slot).start()

    ld_vals.wait()
    for b in range(H // 384):
        vt = vals_v[:, b * 384:(b + 1) * 384].T
        for q in range(8):
            s = b * 8 + q
            zz, ll, cc = s // 4, (s // 2) % 2, s % 2
            vts[cc, pl.ds(zz * ZROWS + ll * ROWS, ROWS), :] = vt[q * ROWS:(q + 1) * ROWS]
    cp_a2 = rcopy(vts.at[oc], a2.at[:, pl.ds(TOK, TOK)], a2_s, a2_r, core_dev)
    cp_a2.start()
    a2[:, pl.ds(0, TOK)] = vts[core]

    for r in range(1, CLIPS):
        c = lax.rem(clip + r, CLIPS)
        rcopy(rsb, rrb.at[c], r_s.at[r - 1], r_r.at[c], (c, seq)).wait_recv()
    total = rrb[0]
    for c in range(1, CLIPS):
        total = total + rrb[c]
    adv = rrb[clip] - total / CLIPS
    advb[...] = adv
    adv1 = adv[0:1, 0:1]
    gadv[...] = gate_ref[...] * adv1

    ld_cot.wait()
    cp_cot.wait_recv()
    cp_a2.wait_recv()

    zl_dev = dev(x, h, lo, zr(sgn), core)
    zs_dev = dev(x, h, lo, zr(-sgn), core)

    def zlong(t, k):
        return rcopy(zls.at[t, k], zlr.at[t, k], zl_s.at[t * NC + k], zl_r.at[t * NC + k], zl_dev)

    def zshort(t, k):
        return rcopy(zss.at[t, k], zsr.at[t, k], zs_s.at[t * NC + k], zs_r.at[t * NC + k], zs_dev)

    def block(k, d):
        return gs[k, pl.ds(pl.multiple_of(d * ZROWS, ZROWS), ZROWS), :]

    def zstep(t, k):
        d = zr(sgn * (4 - t))
        if t == 0:
            zls[t, k] = block(k, d).astype(BF16)
        else:
            zlong(t - 1, k).wait_recv()
            zls[t, k] = (block(k, d) + zlr[t - 1, k].astype(F32)).astype(BF16)
        zlong(t, k).start()
        if t < 3:
            d = zr(-sgn * (3 - t))
            if t == 0:
                zss[t, k] = block(k, d).astype(BF16)
            else:
                zshort(t - 1, k).wait_recv()
                zss[t, k] = (block(k, d) + zsr[t - 1, k].astype(F32)).astype(BF16)
            zshort(t, k).start()

    def g_chunk(k):
        def tile(j, carry):
            off = pl.multiple_of(j * TILE, TILE)
            cols = pl.ds(pl.multiple_of(k * CC + j * TILE, TILE), TILE)
            g = jnp.dot(a2[...], cot2[:, cols], preferred_element_type=F32)
            gs[k, :, pl.ds(off, TILE)] = g[:HALF] * gadv[:, cols]
            es[:, cols] = g[HALF:] * advb[0:1, 0:1]
            return carry
        lax.fori_loop(0, CC // TILE, tile, 0)

    def f_copy(q):
        to = (q // 2, z * 4 + (q % 2) * 2 + core)
        return rcopy(fs.at[q], fr.at[me16], f_s.at[q], f_r.at[me16], to)

    def final(k):
        zlong(3, k).wait_recv()
        zshort(2, k).wait_recv()
        r = block(k, z) + zlr[3, k].astype(F32) + zsr[2, k].astype(F32)
        for j in range(2):
            for l in range(2):
                q = (2 * k + j) * 2 + l
                fs[q] = r[l * ROWS:(l + 1) * ROWS, j * SL:(j + 1) * SL].astype(BF16)

                @pl.when(me16 != q)
                def _():
                    f_copy(q).start()

    def w_use(slot, first=False, own=False):
        if own:
            ld_w0.wait()
            ld_w1.wait()
        else:
            w_core_other(slot).wait_recv()
        cols = pl.ds(pl.multiple_of(slot * SL, SL), SL)
        proj = jnp.dot(vals_v[:, :HALF], wf[slot, 0], preferred_element_type=F32)
        proj = proj + jnp.dot(vals_v[:, HALF:], wf[slot, 1], preferred_element_type=F32)
        emb = jnp.dot(samp_t[...], ew_ref[:, cols], preferred_element_type=F32)
        bo_ref[:, cols] = (emb + gate_ref[:, cols] * proj).astype(BF16)
        br = branch[:, cols]
        for i in range(2):
            g = lax.dot_general(br, wf[slot, i], (((1,), (1,)), ((), ())), preferred_element_type=F32)
            if first:
                ga_acc[:, i * HALF:(i + 1) * HALF] = g
            else:
                ga_acc[:, i * HALF:(i + 1) * HALF] += g

    me4 = core * 2 + lo

    def e1_copy():
        return rcopy(e1s, e1r, e1_s, e1_r, side)

    def e2_copy(r):
        return rcopy(e2s.at[zr(r)], e2r.at[z], e2_s.at[r - 1], e2_r.at[z], dev(x, h, lo, zr(r), core))

    def e3_copy(r):
        return rcopy(ef.at[me4, z], ef.at[me4, z], e3_s.at[r - 1], e3_r.at[z], dev(x, h, lo, zr(r), core))

    def e4_copy(i):
        to = [side, core_dev, dev(x, h, olo, z, oc)][i]
        return rcopy(ef.at[me4], ef.at[me4], e4_s.at[i], e4_r.at[me4], to)

    def e_one():
        e1s[...] = es[pl.ds(pl.multiple_of(olo * 16, 16), 16), :].astype(BF16)
        e1_copy().start()

    def e_two():
        e1_copy().wait_recv()
        part = es[pl.ds(pl.multiple_of(lo * 16, 16), 16), :] + e1r[...].astype(F32)
        for d in range(NZ):
            e2s[d] = part[:, d * SL:(d + 1) * SL].astype(BF16)
        for r in range(1, NZ):
            e2_copy(r).start()
        e2r[z] = e2s[z]

    def e_three():
        for r in range(1, NZ):
            o = zr(r)
            rcopy(e2s.at[o], e2r.at[o], e2_s.at[r - 1], e2_r.at[o], dev(x, h, lo, o, core)).wait_recv()
        tot = e2r[0].astype(F32)
        for d in range(1, NZ):
            tot = tot + e2r[d].astype(F32)
        ef[me4, z] = tot.astype(BF16)
        for r in range(1, NZ):
            e3_copy(r).start()

    def e_four():
        for r in range(1, NZ):
            o = zr(r)
            rcopy(ef.at[me4, o], ef.at[me4, o], e3_s.at[r - 1], e3_r.at[o], dev(x, h, lo, o, core)).wait_recv()
        for i in range(3):
            e4_copy(i).start()

    def e_five():
        for i, q in enumerate((core * 2 + olo, oc * 2 + lo, oc * 2 + olo)):
            rcopy(ef.at[q], ef.at[q], e4_s.at[i], e4_r.at[q], side).wait_recv()
        for q in range(4):
            for d in range(NZ):
                ge_ref[q * 16:(q + 1) * 16, d * SL:(d + 1) * SL] = ef[q, d].astype(F32)

    def y_c(i):
        w_fwd(a_slot(i), wy_s.at[i], cross).start()

    def y_r(i):
        got(b_slot(i))
        w_fwd(b_slot(i), wy_s.at[i], side).start()

    def stage_xa():
        got(a_slot(1))
        got(a_slot(3))
        w_fwd(h * NX + xr(-sgn), wx_s.at[2], dev(xr(sgn), h, lo, z, core)).start()

        @pl.when(role_c)
        def _():
            y_c(1)
            y_c(3)

    def stage_xb():
        got(a_slot(2))

        @pl.when(role_c)
        def _():
            y_c(2)

    def stage_r(i):
        @pl.when(role_r)
        def _():
            y_r(i)

    def stage_c(i):
        @pl.when(role_c)
        def _():
            got(b_slot(i))

    for k in range(NC):
        g_chunk(k)
        zstep(0, k)
    e_one()
    stage_r(0)
    scaled = (cot2[pl.ds(0, TOK), :].astype(F32) * advb[0:1, 0:1]).astype(BF16)
    branch[...] = (scaled.astype(F32) * gate_ref[...]).astype(BF16)

    zstep(1, 0)
    e_two()
    w_use(clip, first=True, own=True)
    zstep(1, 1)
    stage_xa()
    stage_c(0)
    zstep(1, 2)
    w_use(b_slot(0))
    e_three()
    zstep(1, 3)
    w_use(a_slot(1))
    zstep(2, 0)
    stage_xb()
    stage_r(1)
    w_use(a_slot(3))
    zstep(2, 1)
    e_four()
    w_use(a_slot(2))
    zstep(2, 2)
    stage_r(3)
    stage_c(1)
    zstep(2, 3)
    e_five()
    w_use(b_slot(1))
    zstep(3, 0)
    stage_r(2)
    stage_c(3)
    zstep(3, 1)
    w_use(b_slot(3))
    zstep(3, 2)
    stage_c(2)
    zstep(3, 3)
    w_use(b_slot(2))
    ga_ref[...] = ga_acc[...].astype(BF16)
    for k in range(NC):
        final(k)

    for q in range(16):
        @pl.when(me16 == q)
        def _():
            fr[q] = fs[q]

        @pl.when(me16 != q)
        def _():
            rcopy(fs.at[q], fr.at[q], f_s.at[q], f_r.at[q], core_dev).wait_recv()
    acc = fr[0].astype(F32)
    for q in range(1, 16):
        acc = acc + fr[q].astype(F32)
    gw_ref[...] = acc

    for cp in rsends:
        cp.wait_send()
    cp_cot.wait_send()
    cp_a2.wait_send()
    w_own(wx_s.at[0], xp).wait_send()
    w_own(wx_s.at[1], xm).wait_send()
    w_fwd(a_slot(1), wx_s.at[2], xp).wait_send()
    for i in range(4):
        w_fwd(a_slot(1), wy_s.at[i], side).wait_send()
    for i in range(1, 4):
        w_core(a_slot(i)).wait_send()
    for i in range(4):
        w_core(b_slot(i)).wait_send()
    for t in range(4):
        for k in range(NC):
            zlong(t, k).wait_send()
            if t < 3:
                zshort(t, k).wait_send()
    for q in range(16):
        @pl.when(me16 != q)
        def _():
            f_copy(q).wait_send()
    e1_copy().wait_send()
    for r in range(1, NZ):
        e2_copy(r).wait_send()
        e3_copy(r).wait_send()
    for i in range(3):
        e4_copy(i).wait_send()


def fused(step, rewards, lat, noi, vc, vu, ew, gate, vals, w, cot):
    vm = pl.BlockSpec(memory_space=pltpu.VMEM)
    sm = pl.BlockSpec(memory_space=pltpu.SMEM)
    anyspace = pl.BlockSpec(memory_space=pl.ANY)
    dma = pltpu.SemaphoreType.DMA
    scratch = [
        pltpu.VMEM((TOK, H), BF16),
        pltpu.VMEM((2 * TOK, D), BF16),
        pltpu.VMEM((HALF + 32, 2 * TOK), BF16),
        pltpu.VMEM((2, HALF + 32, TOK), BF16),
        pltpu.VMEM((CLIPS, 2, HALF, SL), BF16),
        pltpu.VMEM((NC, HALF, CC), F32),
        pltpu.VMEM((32, D), F32),
        pltpu.VMEM((4, NC, ZROWS, CC), BF16),
        pltpu.VMEM((4, NC, ZROWS, CC), BF16),
        pltpu.VMEM((3, NC, ZROWS, CC), BF16),
        pltpu.VMEM((3, NC, ZROWS, CC), BF16),
        pltpu.VMEM((16, ROWS, SL), BF16),
        pltpu.VMEM((16, ROWS, SL), BF16),
        pltpu.VMEM((16, D), BF16),
        pltpu.VMEM((16, D), BF16),
        pltpu.VMEM((NZ, 16, SL), BF16),
        pltpu.VMEM((NZ, 16, SL), BF16),
        pltpu.VMEM((4, NZ, 16, SL), BF16),
        pltpu.VMEM((8, 128), F32),
        pltpu.VMEM((CLIPS, 8, 128), F32),
        pltpu.VMEM((TOK, CH), BF16),
        pltpu.VMEM((TOK, D), BF16),
        pltpu.VMEM((1, D), F32),
        pltpu.VMEM((8, 128), F32),
        pltpu.VMEM((TOK, H), F32),
        dma((4,)), dma((7,)), dma((8,)), dma, dma, dma, dma,
        dma((3,)), dma((4,)), dma((8,)), dma((8,)), dma((8,)),
        dma((4 * NC,)), dma((4 * NC,)), dma((3 * NC,)), dma((3 * NC,)),
        dma((16,)), dma((16,)), dma, dma,
        dma((7,)), dma((8,)), dma((7,)), dma((8,)), dma((3,)), dma((4,)),
    ]
    return pl.pallas_call(
        kernel,
        name="fused_step",
        out_shape=(
            jax.ShapeDtypeStruct((TOK, D), BF16),
            jax.ShapeDtypeStruct((TOK, H), BF16),
            jax.ShapeDtypeStruct((ROWS, SL), F32),
            jax.ShapeDtypeStruct((CH, D), F32),
        ),
        in_specs=[sm, sm, vm, vm, vm, vm, vm, vm, anyspace, anyspace, anyspace],
        out_specs=(vm, vm, vm, vm),
        scratch_shapes=scratch,
        compiler_params=pltpu.CompilerParams(
            collective_id=0, has_side_effects=True, vmem_limit_bytes=58 * 2**20
        ),
    )(step, rewards, lat, noi, vc, vu, ew, gate, vals, w, cot)


def local(latent, sample_noise, vel_cond, vel_uncond, step_index, embed_w, gate_scale, attn_vals, out_w, cotangent, rewards):
    bo, ga, gw, ge = fused(
        step_index, rewards, latent[0], sample_noise[0], vel_cond[0], vel_uncond[0], embed_w,
        gate_scale, attn_vals[0], out_w, cotangent[0],
    )
    return bo[None], ga[None], gw, ge[None]


def solution(mesh):
    in_specs = (
        P("clip", None, "seq"),
        P("clip", None, "seq"),
        P("clip", None, "seq"),
        P("clip", None, "seq"),
        P(),
        P(),
        P("clip", None),
        P("clip", "seq", None),
        P(None, "clip"),
        P("clip", "seq", None),
        P("clip"),
    )
    out_specs = (
        P("clip", "seq", None),
        P("clip", "seq", None),
        P("seq", "clip"),
        P("clip", None, None),
    )
    return jax.shard_map(local, mesh=mesh, in_specs=in_specs, out_specs=out_specs, check_vma=False)
```

```python
import jax
import jax.numpy as jnp
from jax import lax
from jax.experimental import pallas as pl
from jax.experimental.pallas import tpu as pltpu
from jax.sharding import PartitionSpec as P

NSTEPS = 16
SHIFT_FACTOR = 7.0
GUIDANCE = 6.0
NOISE_LEVEL = 0.3

D = 3072
H = 1536
CH = 64
TOK = 256
NX, NZ = 4, 8
CLIPS = 8
SL = D // CLIPS
HALF = H // 2
ROWS = 48
ZROWS = 2 * ROWS
NC = 4
CC = D // NC
TILE = 256
QR = H // 4
NARROW = 2 * SL // 3
THIRD = SL - NARROW
ZW = 2 * NARROW
SW = CLIPS * THIRD + 128
MESH = pl.DeviceIdType.MESH
F32, BF16 = jnp.float32, jnp.bfloat16


def sigma_level(index):
    tval = 1.0 - index.astype(F32) / NSTEPS
    return SHIFT_FACTOR * tval / (1.0 + (SHIFT_FACTOR - 1.0) * tval)


def dev(x, h, lo, z, core):
    return (h * NX + x, z * 4 + lo * 2 + core)


def kernel(
    step_ref, rew_ref, lat_ref, noi_ref, vc_ref, vu_ref, ew_ref, gate_ref, vals_ref, w_ref, cot_ref,
    bo_out, ga_out, gw_out, ge_out,
    vals_v, cot2, a2, vts, wf, gs, es, zls, zlr, zss, zsr, fs, fr, fss, frs, ef,
    sss, ssr, szls, szlr, szss, szsr,
    e_own, eo, er, gside, rsb, rrb, samp, samp_t, branch, gadv, advb, ga_acc, bo_ref, ga_ref, gw_ref, ge_ref,
    loc, r_s, r_r, cot_s, cot_r, a2_s, a2_r, wx_s, wy_s, wc_s, w_r, wc_r,
    ss_s, ss_r, szl_s, szl_r, szs_s, szs_r, zl_s, zl_r, zs_s, zs_r, f_s, f_r, f2_s, f2_r, e1_s, e1_r, e3_s, e3_r, e4_s, e4_r,
):
    clip = lax.axis_index("clip")
    seq = lax.axis_index("seq")
    h, x = lax.div(clip, NX), lax.rem(clip, NX)
    z, lo, core = lax.div(seq, 4), lax.rem(lax.div(seq, 2), 2), lax.rem(seq, 2)
    oc, olo, oh = 1 - core, 1 - lo, 1 - h
    sgn = 1 - 2 * core

    def xr(n):
        return lax.rem(x + n + NX, NX)

    def zr(n):
        return lax.rem(z + n + NZ, NZ)

    def rcopy(src, dst, ss, rs, to):
        return pltpu.make_async_remote_copy(
            src_ref=src, dst_ref=dst, send_sem=ss, recv_sem=rs, device_id=to, device_id_type=MESH
        )

    ld_vals = pltpu.make_async_copy(vals_ref, vals_v, loc.at[0])
    ld_cot = pltpu.make_async_copy(cot_ref, cot2.at[pl.ds(0, TOK)], loc.at[1])
    ld_w = pltpu.make_async_copy(w_ref, wf.at[clip], loc.at[2])
    ld_vals.start()
    ld_cot.start()
    ld_w.start()

    bar = pltpu.get_barrier_semaphore()
    me16 = clip * 2 + lo
    partners = []
    for r in range(1, 16):
        o = lax.rem(me16 + r, 16)
        oclip, olo_ = lax.div(o, 2), lax.rem(o, 2)
        partners.append((oclip, z * 4 + olo_ * 2 + core))
    for r in range(1, NZ):
        partners.append(dev(x, h, lo, zr(r), core))
    partners.append(dev(x, h, lo, z, oc))
    partners.append(dev(x, h, olo, z, oc))
    for p in partners:
        pl.semaphore_signal(bar, inc=1, device_id=p, device_id_type=MESH)

    rsb[...] = jnp.full((8, 128), rew_ref[0], F32)
    rrb[clip] = jnp.full((8, 128), rew_ref[0], F32)
    idx = jnp.full((1, TOK), step_ref[0], jnp.int32)
    sig_now = sigma_level(idx)
    sig_next = sigma_level(idx + 1)
    uncond = vu_ref[...].astype(F32)
    guided = uncond + GUIDANCE * (vc_ref[...].astype(F32) - uncond)
    spread = NOISE_LEVEL * jnp.sqrt(sig_now - sig_next)
    sampled = lat_ref[...] + (sig_next - sig_now) * guided + spread * noi_ref[...]
    samp_t[...] = sampled.T.astype(BF16)
    samp_b = sampled.astype(BF16)
    samp[...] = samp_b

    ld_vals.wait()
    for b in range(H // 384):
        vt = vals_v[:, b * 384:(b + 1) * 384].T
        for q in range(8):
            s = b * 8 + q
            zz, ll, cc = s // 4, (s // 2) % 2, s % 2
            vts[cc, pl.ds(zz * ZROWS + ll * ROWS, ROWS), :] = vt[q * ROWS:(q + 1) * ROWS]
    a2[:, pl.ds(0, TOK)] = vts[core]

    pl.semaphore_wait(bar, len(partners))

    core_dev = dev(x, h, lo, z, oc)
    cp_a2 = rcopy(vts.at[oc], a2.at[:, pl.ds(TOK, TOK)], a2_s, a2_r, core_dev)
    cp_a2.start()
    cp_cot = []
    for k in range(NC):
        cols = pl.ds(k * CC, CC)
        cp = rcopy(cot_ref.at[:, cols], cot2.at[pl.ds(TOK, TOK), cols], cot_s.at[k], cot_r.at[k], core_dev)
        cp.start()
        cp_cot.append(cp)
    rsends = []
    for r in range(1, CLIPS):
        c = lax.rem(clip + r, CLIPS)
        cp = rcopy(rsb, rrb.at[clip], r_s.at[r - 1], r_r.at[clip], (c, seq))
        cp.start()
        rsends.append(cp)

    side = dev(x, h, olo, z, core)
    cross = dev(x, oh, olo, z, core)

    def quarter(i):
        return pl.ds(pl.multiple_of((core * 2 + i) * QR, QR), QR)

    def w_own(i, ss, to):
        return rcopy(w_ref.at[quarter(i)], wf.at[clip, quarter(i)], ss, w_r.at[clip * 2 + i], to)

    def w_fwd(slot, i, ss, to):
        return rcopy(wf.at[slot, quarter(i)], wf.at[slot, quarter(i)], ss, w_r.at[slot * 2 + i], to)

    xp = dev(xr(1), h, lo, z, core)
    xm = dev(xr(-1), h, lo, z, core)
    xs = dev(xr(sgn), h, lo, z, core)
    for i in range(2):
        w_own(i, wx_s.at[2 * i], xp).start()
        w_own(i, wx_s.at[2 * i + 1], xm).start()
        w_own(i, wy_s.at[i], cross).start()

    def a_slot(i):
        return h * NX + xr(i)

    def b_slot(i):
        return oh * NX + xr(i)

    def w_core(slot, i):
        n = slot * 2 + i
        return rcopy(wf.at[slot, quarter(i)], wf.at[slot, quarter(i)], wc_s.at[n], wc_r.at[n], core_dev)

    def w_core_other(slot, i):
        n = slot * 2 + i
        rows = pl.ds(pl.multiple_of((oc * 2 + i) * QR, QR), QR)
        return rcopy(wf.at[slot, rows], wf.at[slot, rows], wc_s.at[n], wc_r.at[n], core_dev)

    def got(slot, i):
        w_fwd(slot, i, wx_s.at[0], xp).wait_recv()
        w_core(slot, i).start()

    ld_cot.wait()

    zl_dev = dev(x, h, lo, zr(sgn), core)
    zs_dev = dev(x, h, lo, zr(-sgn), core)

    def zlong(t, k):
        n = t * NC + k
        return rcopy(zls.at[t, k], zlr.at[t, k], zl_s.at[n], zl_r.at[n], zl_dev)

    def zshort(t, k):
        n = t * NC + k
        return rcopy(zss.at[t, k], zsr.at[t, k], zs_s.at[n], zs_r.at[n], zs_dev)

    def zrows(d):
        return pl.ds(pl.multiple_of(d * ZROWS, ZROWS), ZROWS)

    def zadd(t, k, d, out, got_ref):
        v = gs[k, zrows(d), :]
        if t:
            v = v + got_ref[t - 1, k].astype(F32)
        out[t, k] = v.astype(BF16)

    def zstep(t, k):
        if t:
            zlong(t - 1, k).wait_recv()
        zadd(t, k, zr(sgn * (4 - t)), zls, zlr)
        zlong(t, k).start()
        if t < 3:
            if t:
                zshort(t - 1, k).wait_recv()
            zadd(t, k, zr(-sgn * (3 - t)), zss, zsr)
            zshort(t, k).start()

    def lrows(d, l):
        return pl.ds(pl.multiple_of(d * ZROWS + l * ROWS, ROWS), ROWS)

    def sown(d, l):
        emb = []
        for i in range(3):
            cols = pl.ds(pl.multiple_of(d * SL + i * 128, 128), 128)
            emb.append(es[pl.ds(pl.multiple_of(l * 16, 16), 16), cols])
        return jnp.concatenate([gside[lrows(d, l), :], jnp.concatenate(emb, axis=0)], axis=1)

    sorder = (sgn * 4, -sgn * 3, sgn * 3, -sgn * 2, sgn * 2, -sgn, sgn, 0)

    me4 = core * 2 + lo

    def e3_copy(r):
        return rcopy(ef.at[me4, z], ef.at[me4, z], e3_s.at[r - 1], e3_r.at[z], dev(x, h, lo, zr(r), core))

    def e4_copy(i):
        to = [side, core_dev, dev(x, h, olo, z, oc)][i]
        return rcopy(ef.at[me4], ef.at[me4], e4_s.at[i], e4_r.at[me4], to)

    def fs_copy(j):
        return rcopy(fss.at[j], frs.at[clip], f2_s.at[j], f2_r.at[clip], (j, seq))

    def side_copy(i):
        return rcopy(sss.at[i], ssr.at[i], ss_s.at[i], ss_r.at[i], side)

    def side_send():
        for i, n in enumerate(sorder):
            sss[i] = sown(zr(n), olo).astype(BF16)
            side_copy(i).start()

    def slong(t):
        return rcopy(szls.at[t], szlr.at[t], szl_s.at[t], szl_r.at[t], zl_dev)

    def sshort(t):
        return rcopy(szss.at[t], szsr.at[t], szs_s.at[t], szs_r.at[t], zs_dev)

    def sstep(t):
        side_copy(2 * t).wait_recv()
        v = sown(zr(sgn * (4 - t)), lo) + ssr[2 * t].astype(F32)
        if t:
            slong(t - 1).wait_recv()
            v = v + szlr[t - 1].astype(F32)
        szls[t] = v.astype(BF16)
        slong(t).start()
        if t < 3:
            side_copy(2 * t + 1).wait_recv()
            v = sown(zr(-sgn * (3 - t)), lo) + ssr[2 * t + 1].astype(F32)
            if t:
                sshort(t - 1).wait_recv()
                v = v + szsr[t - 1].astype(F32)
            szss[t] = v.astype(BF16)
            sshort(t).start()

    def sfinal():
        side_copy(7).wait_recv()
        slong(3).wait_recv()
        sshort(2).wait_recv()
        v = sown(z, lo) + ssr[7].astype(F32) + szlr[3].astype(F32) + szsr[2].astype(F32)
        for j in range(CLIPS):
            o = j * SL + NARROW
            fss[j] = (v[:, j * THIRD:(j + 1) * THIRD] * gadv[:, o:o + THIRD]).astype(BF16)

            @pl.when(clip != j)
            def _():
                fs_copy(j).start()
        emb = v[:, CLIPS * THIRD:].astype(BF16)
        ef[me4, z] = jnp.concatenate([emb[i * 16:(i + 1) * 16] for i in range(3)], axis=1)
        for r in range(1, NZ):
            e3_copy(r).start()

    def advantage():
        for r in range(1, CLIPS):
            c = lax.rem(clip + r, CLIPS)
            rcopy(rsb, rrb.at[c], r_s.at[r - 1], r_r.at[c], (c, seq)).wait_recv()
        total = rrb[0]
        for c in range(1, CLIPS):
            total = total + rrb[c]
        adv = rrb[clip] - total / CLIPS
        advb[...] = adv
        adv1 = adv[0:1, 0:1]
        gadv[...] = gate_ref[...] * adv1

    def e_first():
        def tile(j, carry):
            cols = pl.ds(pl.multiple_of(j * TILE, TILE), TILE)
            g = jnp.dot(samp[...], cot2[pl.ds(0, TOK), cols], preferred_element_type=F32)
            e_own[:, cols] = g
            eo[:, cols] = g.astype(BF16)
            return carry
        lax.fori_loop(0, D // TILE, tile, 0)
        e1_copy().start()

    def e1_copy():
        rows = pl.ds(pl.multiple_of(oc * 32, 32), 32)
        return rcopy(eo.at[rows], er, e1_s, e1_r, core_dev)

    def e_sum():
        e1_copy().wait_recv()
        es[...] = e_own[pl.ds(pl.multiple_of(core * 32, 32), 32), :] + er[...].astype(F32)

    def g_chunk(k):
        def tile(j, carry):
            cols = pl.ds(pl.multiple_of((2 * k + j) * SL, 128), NARROW)
            g = jnp.dot(a2[...], cot2[:, cols], preferred_element_type=F32)
            gs[k, :, pl.ds(pl.multiple_of(j * NARROW, NARROW), NARROW)] = g
            return carry
        lax.fori_loop(0, 2, tile, 0)

    def g_side():
        def tile(j, carry):
            parts = [cot2[:, pl.ds(pl.multiple_of((2 * j + i) * SL + NARROW, 128), THIRD)] for i in range(2)]
            g = jnp.dot(a2[...], jnp.concatenate(parts, axis=1), preferred_element_type=F32)
            gside[:, pl.ds(pl.multiple_of(j * 2 * THIRD, 2 * THIRD), 2 * THIRD)] = g
            return carry
        lax.fori_loop(0, NC, tile, 0)

    def f_copy(q):
        to = (q // 2, z * 4 + (q % 2) * 2 + core)
        return rcopy(fs.at[q], fr.at[me16], f_s.at[q], f_r.at[me16], to)

    def final(k):
        zlong(3, k).wait_recv()
        zshort(2, k).wait_recv()
        both = gs[k, zrows(z), :] + zlr[3, k].astype(F32) + zsr[2, k].astype(F32)
        for j in range(2):
            r = both[:, j * NARROW:(j + 1) * NARROW] * gadv[:, k * CC + j * SL:k * CC + j * SL + NARROW]
            for l in range(2):
                q = (2 * k + j) * 2 + l
                fs[q] = r[l * ROWS:(l + 1) * ROWS].astype(BF16)

                @pl.when(me16 != q)
                def _():
                    f_copy(q).start()

    def w_use(slot, first=False, own=False):
        if own:
            ld_w.wait()
        else:
            w_core_other(slot, 0).wait_recv()
            w_core_other(slot, 1).wait_recv()
        cols = pl.ds(pl.multiple_of(slot * SL, SL), SL)
        proj = jnp.dot(vals_v[...], wf[slot], preferred_element_type=F32)
        emb = jnp.dot(samp_t[...], ew_ref[:, cols], preferred_element_type=F32)
        bo_ref[:, cols] = (emb + gate_ref[:, cols] * proj).astype(BF16)
        br = branch[:, cols]
        for i in range(2):
            g = lax.dot_general(br, wf[slot, i * HALF:(i + 1) * HALF], (((1,), (1,)), ((), ())), preferred_element_type=F32)
            if first:
                ga_acc[:, i * HALF:(i + 1) * HALF] = g
            else:
                ga_acc[:, i * HALF:(i + 1) * HALF] += g

    def e_four():
        for r in range(1, NZ):
            o = zr(r)
            rcopy(ef.at[me4, o], ef.at[me4, o], e3_s.at[r - 1], e3_r.at[o], dev(x, h, lo, o, core)).wait_recv()
        for i in range(3):
            e4_copy(i).start()

    def e_five():
        for i, q in enumerate((core * 2 + olo, oc * 2 + lo, oc * 2 + olo)):
            rcopy(ef.at[q], ef.at[q], e4_s.at[i], e4_r.at[q], side).wait_recv()
        for q in range(4):
            for d in range(NZ):
                ge_ref[q * 16:(q + 1) * 16, d * SL:(d + 1) * SL] = ef[q, d].astype(F32) * advb[0:1, 0:1]
        pltpu.make_async_copy(ge_ref, ge_out, loc.at[4]).start()

    def stage_1():
        got(a_slot(1), 0)
        got(a_slot(3), 0)
        w_fwd(h * NX + xr(-sgn), 0, wx_s.at[4], xs).start()
        w_fwd(a_slot(1), 0, wy_s.at[2], cross).start()
        w_fwd(a_slot(3), 0, wy_s.at[3], cross).start()

    def stage_2():
        got(a_slot(1), 1)
        got(a_slot(3), 1)
        w_fwd(h * NX + xr(-sgn), 1, wx_s.at[5], xs).start()

    def stage_2b():
        got(b_slot(0), 0)
        got(b_slot(0), 1)
        w_fwd(b_slot(0), 1, wx_s.at[6], xp).start()
        w_fwd(b_slot(0), 1, wx_s.at[7], xm).start()

    def stage_3():
        got(a_slot(2), 0)
        w_fwd(a_slot(2), 0, wy_s.at[4], cross).start()

    def stage_4():
        got(a_slot(2), 1)

    def stage_5(i):
        got(b_slot(i), 0)

    def stage_6():
        got(b_slot(1), 1)
        got(b_slot(3), 1)
        w_fwd(oh * NX + xr(-sgn), 1, wx_s.at[8], xs).start()

    def stage_8():
        got(b_slot(2), 1)

    e_first()
    cp_a2.wait_recv()
    cp_cot[0].wait_recv()
    g_chunk(0)
    zstep(0, 0)
    for k in range(1, NC):
        cp_cot[k].wait_recv()
    g_side()
    e_sum()
    side_send()
    for k in range(1, NC):
        g_chunk(k)
        zstep(0, k)
    zstep(1, 0)
    stage_1()
    advantage()
    scaled = (cot2[pl.ds(0, TOK), :].astype(F32) * advb[0:1, 0:1]).astype(BF16)
    branch[...] = (scaled.astype(F32) * gate_ref[...]).astype(BF16)
    sstep(0)
    zstep(1, 1)
    zstep(1, 2)
    stage_2()
    stage_2b()
    w_use(clip, first=True, own=True)
    zstep(1, 3)
    stage_3()
    w_use(a_slot(1))
    zstep(2, 0)
    stage_5(1)
    w_use(a_slot(3))
    sstep(1)
    zstep(2, 1)
    stage_4()
    w_use(b_slot(0))
    zstep(2, 2)
    w_use(a_slot(2))
    zstep(2, 3)
    zstep(3, 0)
    stage_5(3)
    stage_6()
    w_use(b_slot(1))
    sstep(2)
    zstep(3, 1)
    stage_5(2)
    stage_8()
    w_use(b_slot(3))
    zstep(3, 2)
    zstep(3, 3)
    w_use(b_slot(2))
    pltpu.make_async_copy(bo_ref, bo_out, loc.at[6]).start()
    ga_ref[...] = ga_acc[...].astype(BF16)
    pltpu.make_async_copy(ga_ref, ga_out, loc.at[7]).start()
    final(0)
    sstep(3)
    final(1)
    final(2)
    final(3)
    sfinal()
    e_four()
    e_five()

    fr[me16] = fs[me16]
    frs[clip] = fss[clip]
    for q in range(16):
        @pl.when(me16 != q)
        def _():
            rcopy(fs.at[q], fr.at[q], f_s.at[q], f_r.at[q], core_dev).wait_recv()
    for j in range(CLIPS):
        @pl.when(clip != j)
        def _():
            rcopy(fss.at[j], frs.at[j], f2_s.at[j], f2_r.at[j], core_dev).wait_recv()
    acc = fr[0].astype(F32)
    for q in range(1, 16):
        acc = acc + fr[q].astype(F32)
    gw_ref[:, :NARROW] = acc
    acc = frs[0].astype(F32)
    for j in range(1, CLIPS):
        acc = acc + frs[j].astype(F32)
    gw_ref[:, NARROW:] = acc
    pltpu.make_async_copy(gw_ref, gw_out, loc.at[5]).start()

    pltpu.make_async_copy(ge_ref, ge_out, loc.at[4]).wait()
    pltpu.make_async_copy(gw_ref, gw_out, loc.at[5]).wait()
    pltpu.make_async_copy(bo_ref, bo_out, loc.at[6]).wait()
    pltpu.make_async_copy(ga_ref, ga_out, loc.at[7]).wait()
    for cp in rsends:
        cp.wait_send()
    for cp in cp_cot:
        cp.wait_send()
    cp_a2.wait_send()
    for n in range(9):
        w_fwd(a_slot(1), 0, wx_s.at[n], xp).wait_send()
    for n in range(5):
        w_fwd(a_slot(1), 0, wy_s.at[n], side).wait_send()
    for i in range(2):
        for n in range(1, 4):
            w_core(a_slot(n), i).wait_send()
        for n in range(4):
            w_core(b_slot(n), i).wait_send()
    for i in range(NZ):
        side_copy(i).wait_send()
    for t in range(4):
        slong(t).wait_send()
        if t < 3:
            sshort(t).wait_send()
        for k in range(NC):
            zlong(t, k).wait_send()
            if t < 3:
                zshort(t, k).wait_send()
    for q in range(16):
        @pl.when(me16 != q)
        def _():
            f_copy(q).wait_send()
    for j in range(CLIPS):
        @pl.when(clip != j)
        def _():
            fs_copy(j).wait_send()
    e1_copy().wait_send()
    for r in range(1, NZ):
        e3_copy(r).wait_send()
    for i in range(3):
        e4_copy(i).wait_send()


def fused(step, rewards, lat, noi, vc, vu, ew, gate, vals, w, cot):
    vm = pl.BlockSpec(memory_space=pltpu.VMEM)
    sm = pl.BlockSpec(memory_space=pltpu.SMEM)
    anyspace = pl.BlockSpec(memory_space=pl.ANY)
    dma = pltpu.SemaphoreType.DMA
    scratch = [
        pltpu.VMEM((TOK, H), BF16),
        pltpu.VMEM((2 * TOK, D), BF16),
        pltpu.VMEM((HALF, 2 * TOK), BF16),
        pltpu.VMEM((2, HALF, TOK), BF16),
        pltpu.VMEM((CLIPS, H, SL), BF16),
        pltpu.VMEM((NC, HALF, ZW), F32),
        pltpu.VMEM((32, D), F32),
        pltpu.VMEM((4, NC, ZROWS, ZW), BF16),
        pltpu.VMEM((4, NC, ZROWS, ZW), BF16),
        pltpu.VMEM((3, NC, ZROWS, ZW), BF16),
        pltpu.VMEM((3, NC, ZROWS, ZW), BF16),
        pltpu.VMEM((16, ROWS, NARROW), BF16),
        pltpu.VMEM((16, ROWS, NARROW), BF16),
        pltpu.VMEM((CLIPS, ROWS, THIRD), BF16),
        pltpu.VMEM((CLIPS, ROWS, THIRD), BF16),
        pltpu.VMEM((4, NZ, 16, SL), BF16),
        pltpu.VMEM((NZ, ROWS, SW), BF16),
        pltpu.VMEM((NZ, ROWS, SW), BF16),
        pltpu.VMEM((4, ROWS, SW), BF16),
        pltpu.VMEM((4, ROWS, SW), BF16),
        pltpu.VMEM((3, ROWS, SW), BF16),
        pltpu.VMEM((3, ROWS, SW), BF16),
        pltpu.VMEM((CH, D), F32),
        pltpu.VMEM((CH, D), BF16),
        pltpu.VMEM((32, D), BF16),
        pltpu.VMEM((HALF, CLIPS * THIRD), F32),
        pltpu.VMEM((8, 128), F32),
        pltpu.VMEM((CLIPS, 8, 128), F32),
        pltpu.VMEM((CH, TOK), BF16),
        pltpu.VMEM((TOK, CH), BF16),
        pltpu.VMEM((TOK, D), BF16),
        pltpu.VMEM((1, D), F32),
        pltpu.VMEM((8, 128), F32),
        pltpu.VMEM((TOK, H), F32),
        pltpu.VMEM((TOK, D), BF16),
        pltpu.VMEM((TOK, H), BF16),
        pltpu.VMEM((ROWS, SL), F32),
        pltpu.VMEM((CH, D), F32),
        dma((8,)), dma((7,)), dma((8,)), dma((NC,)), dma((NC,)), dma, dma,
        dma((9,)), dma((5,)), dma((16,)), dma((16,)), dma((16,)),
        dma((NZ,)), dma((NZ,)), dma((4,)), dma((4,)), dma((3,)), dma((3,)),
        dma((4 * NC,)), dma((4 * NC,)), dma((3 * NC,)), dma((3 * NC,)),
        dma((16,)), dma((16,)), dma((8,)), dma((8,)), dma, dma, dma((7,)), dma((8,)), dma((3,)), dma((4,)),
    ]
    return pl.pallas_call(
        kernel,
        name="fused_step",
        out_shape=(
            jax.ShapeDtypeStruct((TOK, D), BF16),
            jax.ShapeDtypeStruct((TOK, H), BF16),
            jax.ShapeDtypeStruct((ROWS, SL), F32),
            jax.ShapeDtypeStruct((CH, D), F32),
        ),
        in_specs=[sm, sm, vm, vm, vm, vm, vm, vm, anyspace, anyspace, anyspace],
        out_specs=(anyspace, anyspace, anyspace, anyspace),
        scratch_shapes=scratch,
        compiler_params=pltpu.CompilerParams(
            collective_id=0, has_side_effects=True, vmem_limit_bytes=58 * 2**20
        ),
    )(step, rewards, lat, noi, vc, vu, ew, gate, vals, w, cot)


def copy_kernel(bo, ga, gw, ge, bo_o, ga_o, gw_o, ge_o, v0, v1, v2, v3, ins, outs):
    loads, stores = [], []
    n = 0
    for src, mid, dst, parts in ((bo, v0, bo_o, 4), (ga, v1, ga_o, 2), (ge, v3, ge_o, 2), (gw, v2, gw_o, 1)):
        rows = src.shape[0] // parts
        for p in range(parts):
            at = pl.ds(p * rows, rows)
            loads.append(pltpu.make_async_copy(src.at[at], mid.at[at], ins.at[n]))
            stores.append(pltpu.make_async_copy(mid.at[at], dst.at[at], outs.at[n]))
            n += 1
    for c in loads:
        c.start()
    for a, b in zip(loads, stores):
        a.wait()
        b.start()
    for c in stores:
        c.wait()


def copied(*arrays):
    anyspace = pl.BlockSpec(memory_space=pl.ANY)
    return pl.pallas_call(
        copy_kernel,
        name="results",
        out_shape=tuple(jax.ShapeDtypeStruct(a.shape, a.dtype) for a in arrays),
        in_specs=[anyspace] * 4,
        out_specs=(anyspace,) * 4,
        scratch_shapes=[pltpu.VMEM(a.shape, a.dtype) for a in arrays]
        + [pltpu.SemaphoreType.DMA((9,)), pltpu.SemaphoreType.DMA((9,))],
        compiler_params=pltpu.CompilerParams(vmem_limit_bytes=60 * 2**20),
    )(*arrays)


def local(latent, sample_noise, vel_cond, vel_uncond, step_index, embed_w, gate_scale, attn_vals, out_w, cotangent, rewards):
    bo, ga, gw, ge = copied(*fused(
        step_index, rewards, latent[0], sample_noise[0], vel_cond[0], vel_uncond[0], embed_w,
        gate_scale, attn_vals[0], out_w, cotangent[0],
    ))
    return bo[None], ga[None], gw, ge[None]


def solution(mesh):
    in_specs = (
        P("clip", None, "seq"),
        P("clip", None, "seq"),
        P("clip", None, "seq"),
        P("clip", None, "seq"),
        P(),
        P(),
        P("clip", None),
        P("clip", "seq", None),
        P(None, "clip"),
        P("clip", "seq", None),
        P("clip"),
    )
    out_specs = (
        P("clip", "seq", None),
        P("clip", "seq", None),
        P("seq", "clip"),
        P("clip", None, None),
    )
    return jax.shard_map(local, mesh=mesh, in_specs=in_specs, out_specs=out_specs, check_vma=False)
```

```python
import jax
import jax.numpy as jnp
from jax import lax
from jax.experimental import pallas as pl
from jax.experimental.pallas import tpu as pltpu
from jax.sharding import PartitionSpec as P

NSTEPS = 16
SHIFT_FACTOR = 7.0
GUIDANCE = 6.0
NOISE_LEVEL = 0.3

D = 3072
H = 1536
CH = 64
TOK = 256
NX, NZ = 4, 8
CLIPS = 8
SL = D // CLIPS
HALF = H // 2
ROWS = 48
ZROWS = 2 * ROWS
NC = 4
CC = D // NC
TILE = 256
QR = H // 4
THIRD = SL // 3
ZW = 3 * THIRD
SW = NC * ZW + 128
MESH = pl.DeviceIdType.MESH


def mwidth(j):
    return 2 * THIRD if j % 2 else THIRD


def swidth(j):
    return SL - mwidth(j)


def soffset(j):
    return (j // 4) * 2 * ZW + (0, 2 * THIRD, 4 * THIRD, 3 * THIRD)[j % 4]

F32, BF16 = jnp.float32, jnp.bfloat16


def sigma_level(index):
    tval = 1.0 - index.astype(F32) / NSTEPS
    return SHIFT_FACTOR * tval / (1.0 + (SHIFT_FACTOR - 1.0) * tval)


def dev(x, h, lo, z, core):
    return (h * NX + x, z * 4 + lo * 2 + core)


def kernel(
    step_in, rew_in, lat_in, noi_in, vc_in, vu_in, ew_in, gate_in, vals_ref, w_ref, cot_ref,
    bo_out, ga_out, gw_out, ge_out,
    step_ref, rew_ref, lat_ref, noi_ref, vc_ref, vu_ref, ew_ref, gate_ref, vals_v, cot2, a2, vts, wf, gs, es, zls, zlr, zss, zsr, fs, fr, fss, frs, ef,
    sss, ssr, szls, szlr, szss, szsr,
    e_own, eo, er, gside, rsb, rrb, samp, samp_t, branch, gadv, advb, ga_acc, bo_ref, ga_ref, gw_ref, ge_ref,
    loc, r_s, r_r, cot_s, cot_r, a2_s, a2_r, wx_s, wy_s, wc_s, w_r, wc_r,
    ss_s, ss_r, szl_s, szl_r, szs_s, szs_r, zl_s, zl_r, zs_s, zs_r, f_s, f_r, f2_s, f2_r, e1_s, e1_r, e3_s, e3_r, e4_s, e4_r,
):
    clip = lax.axis_index("clip")
    seq = lax.axis_index("seq")
    h, x = lax.div(clip, NX), lax.rem(clip, NX)
    z, lo, core = lax.div(seq, 4), lax.rem(lax.div(seq, 2), 2), lax.rem(seq, 2)
    oc, olo, oh = 1 - core, 1 - lo, 1 - h
    sgn = 1 - 2 * core

    def xr(n):
        return lax.rem(x + n + NX, NX)

    def zr(n):
        return lax.rem(z + n + NZ, NZ)

    def rcopy(src, dst, ss, rs, to):
        return pltpu.make_async_remote_copy(
            src_ref=src, dst_ref=dst, send_sem=ss, recv_sem=rs, device_id=to, device_id_type=MESH
        )

    bar = pltpu.get_barrier_semaphore()
    me16 = clip * 2 + lo
    partners = []
    for r in range(1, 16):
        o = lax.rem(me16 + r, 16)
        oclip, olo_ = lax.div(o, 2), lax.rem(o, 2)
        partners.append((oclip, z * 4 + olo_ * 2 + core))
    for r in range(1, NZ):
        partners.append(dev(x, h, lo, zr(r), core))
    partners.append(dev(x, h, lo, z, oc))
    partners.append(dev(x, h, olo, z, oc))
    for p in partners:
        pl.semaphore_signal(bar, inc=1, device_id=p, device_id_type=MESH)

    ld_vals = pltpu.make_async_copy(vals_ref, vals_v, loc.at[0])
    ld_cot = pltpu.make_async_copy(cot_ref, cot2.at[pl.ds(0, TOK)], loc.at[1])
    ld_w = pltpu.make_async_copy(w_ref, wf.at[clip], loc.at[2])
    ld_vals.start()
    ld_cot.start()
    ld_w.start()
    small = ((step_in, step_ref), (rew_in, rew_ref), (lat_in, lat_ref), (noi_in, noi_ref),
             (vc_in, vc_ref), (vu_in, vu_ref), (ew_in, ew_ref), (gate_in, gate_ref))
    ld_small = [pltpu.make_async_copy(a, b, loc.at[8 + i]) for i, (a, b) in enumerate(small)]
    for cp in ld_small:
        cp.start()

    for cp in ld_small[:6]:
        cp.wait()
    rsb[...] = jnp.full((8, 128), rew_ref[0], F32)
    rrb[clip] = jnp.full((8, 128), rew_ref[0], F32)
    idx = jnp.full((1, TOK), step_ref[0], jnp.int32)
    sig_now = sigma_level(idx)
    sig_next = sigma_level(idx + 1)
    uncond = vu_ref[...].astype(F32)
    guided = uncond + GUIDANCE * (vc_ref[...].astype(F32) - uncond)
    spread = NOISE_LEVEL * jnp.sqrt(sig_now - sig_next)
    sampled = lat_ref[...] + (sig_next - sig_now) * guided + spread * noi_ref[...]
    samp_t[...] = sampled.T.astype(BF16)
    samp_b = sampled.astype(BF16)
    samp[...] = samp_b

    ld_vals.wait()
    for b in range(H // 384):
        vt = vals_v[:, b * 384:(b + 1) * 384].T
        for q in range(8):
            s = b * 8 + q
            zz, ll, cc = s // 4, (s // 2) % 2, s % 2
            vts[cc, pl.ds(zz * ZROWS + ll * ROWS, ROWS), :] = vt[q * ROWS:(q + 1) * ROWS]
    a2[:, pl.ds(0, TOK)] = vts[core]

    pl.semaphore_wait(bar, len(partners))

    core_dev = dev(x, h, lo, z, oc)
    cp_a2 = rcopy(vts.at[oc], a2.at[:, pl.ds(TOK, TOK)], a2_s, a2_r, core_dev)
    cp_a2.start()
    cp_cot = []
    for k in range(NC):
        cols = pl.ds(k * CC, CC)
        cp = rcopy(cot_ref.at[:, cols], cot2.at[pl.ds(TOK, TOK), cols], cot_s.at[k], cot_r.at[k], core_dev)
        cp.start()
        cp_cot.append(cp)
    rsends = []
    for r in range(1, CLIPS):
        c = lax.rem(clip + r, CLIPS)
        cp = rcopy(rsb, rrb.at[clip], r_s.at[r - 1], r_r.at[clip], (c, seq))
        cp.start()
        rsends.append(cp)

    side = dev(x, h, olo, z, core)
    cross = dev(x, oh, olo, z, core)

    def quarter(i):
        return pl.ds(pl.multiple_of((core * 2 + i) * QR, QR), QR)

    def w_own(i, ss, to):
        return rcopy(w_ref.at[quarter(i)], wf.at[clip, quarter(i)], ss, w_r.at[clip * 2 + i], to)

    def w_fwd(slot, i, ss, to):
        return rcopy(wf.at[slot, quarter(i)], wf.at[slot, quarter(i)], ss, w_r.at[slot * 2 + i], to)

    xp = dev(xr(1), h, lo, z, core)
    xm = dev(xr(-1), h, lo, z, core)
    xs = dev(xr(sgn), h, lo, z, core)
    for i in range(2):
        w_own(i, wx_s.at[2 * i], xp).start()
        w_own(i, wx_s.at[2 * i + 1], xm).start()
        w_own(i, wy_s.at[i], cross).start()

    def a_slot(i):
        return h * NX + xr(i)

    def b_slot(i):
        return oh * NX + xr(i)

    def w_core(slot, i):
        n = slot * 2 + i
        return rcopy(wf.at[slot, quarter(i)], wf.at[slot, quarter(i)], wc_s.at[n], wc_r.at[n], core_dev)

    def w_core_other(slot, i):
        n = slot * 2 + i
        rows = pl.ds(pl.multiple_of((oc * 2 + i) * QR, QR), QR)
        return rcopy(wf.at[slot, rows], wf.at[slot, rows], wc_s.at[n], wc_r.at[n], core_dev)

    def got(slot, i):
        w_fwd(slot, i, wx_s.at[0], xp).wait_recv()
        w_core(slot, i).start()

    ld_cot.wait()

    zl_dev = dev(x, h, lo, zr(sgn), core)
    zs_dev = dev(x, h, lo, zr(-sgn), core)

    def zlong(t, k):
        n = t * NC + k
        return rcopy(zls.at[t, k], zlr.at[t, k], zl_s.at[n], zl_r.at[n], zl_dev)

    def zshort(t, k):
        n = t * NC + k
        return rcopy(zss.at[t, k], zsr.at[t, k], zs_s.at[n], zs_r.at[n], zs_dev)

    def zrows(d):
        return pl.ds(pl.multiple_of(d * ZROWS, ZROWS), ZROWS)

    def zadd(t, k, d, out, got_ref):
        v = gs[k, zrows(d), :]
        if t:
            v = v + got_ref[t - 1, k].astype(F32)
        out[t, k] = v.astype(BF16)

    def zstep(t, k):
        if t:
            zlong(t - 1, k).wait_recv()
        zadd(t, k, zr(sgn * (4 - t)), zls, zlr)
        zlong(t, k).start()
        if t < 3:
            if t:
                zshort(t - 1, k).wait_recv()
            zadd(t, k, zr(-sgn * (3 - t)), zss, zsr)
            zshort(t, k).start()

    def lrows(d, l):
        return pl.ds(pl.multiple_of(d * ZROWS + l * ROWS, ROWS), ROWS)

    def sown(d, l):
        emb = []
        for i in range(3):
            cols = pl.ds(pl.multiple_of(d * SL + i * 128, 128), 128)
            emb.append(es[pl.ds(pl.multiple_of(l * 16, 16), 16), cols])
        return jnp.concatenate([gside[lrows(d, l), :], jnp.concatenate(emb, axis=0)], axis=1)

    sorder = (sgn * 4, -sgn * 3, sgn * 3, -sgn * 2, sgn * 2, -sgn, sgn, 0)

    me4 = core * 2 + lo

    def e3_copy(r):
        return rcopy(ef.at[me4, z], ef.at[me4, z], e3_s.at[r - 1], e3_r.at[z], dev(x, h, lo, zr(r), core))

    def e4_copy(i):
        to = [side, core_dev, dev(x, h, olo, z, oc)][i]
        return rcopy(ef.at[me4], ef.at[me4], e4_s.at[i], e4_r.at[me4], to)

    def fs_copy(j):
        w = pl.ds(0, swidth(j))
        return rcopy(fss.at[j, :, w], frs.at[clip, :, w], f2_s.at[j], f2_r.at[clip], (j, seq))

    def side_copy(i):
        return rcopy(sss.at[i], ssr.at[i], ss_s.at[i], ss_r.at[i], side)

    def side_send():
        for i, n in enumerate(sorder):
            sss[i] = sown(zr(n), olo).astype(BF16)
            side_copy(i).start()

    def slong(t):
        return rcopy(szls.at[t], szlr.at[t], szl_s.at[t], szl_r.at[t], zl_dev)

    def sshort(t):
        return rcopy(szss.at[t], szsr.at[t], szs_s.at[t], szs_r.at[t], zs_dev)

    def sstep(t):
        side_copy(2 * t).wait_recv()
        v = sown(zr(sgn * (4 - t)), lo) + ssr[2 * t].astype(F32)
        if t:
            slong(t - 1).wait_recv()
            v = v + szlr[t - 1].astype(F32)
        szls[t] = v.astype(BF16)
        slong(t).start()
        if t < 3:
            side_copy(2 * t + 1).wait_recv()
            v = sown(zr(-sgn * (3 - t)), lo) + ssr[2 * t + 1].astype(F32)
            if t:
                sshort(t - 1).wait_recv()
                v = v + szsr[t - 1].astype(F32)
            szss[t] = v.astype(BF16)
            sshort(t).start()

    def sfinal():
        side_copy(7).wait_recv()
        slong(3).wait_recv()
        sshort(2).wait_recv()
        v = sown(z, lo) + ssr[7].astype(F32) + szlr[3].astype(F32) + szsr[2].astype(F32)
        for j in range(CLIPS):
            o, w, c = j * SL + mwidth(j), swidth(j), soffset(j)
            fss[j, :, :w] = (v[:, c:c + w] * gadv[:, o:o + w]).astype(BF16)

            @pl.when(clip != j)
            def _():
                fs_copy(j).start()
        emb = v[:, NC * ZW:].astype(BF16)
        ef[me4, z] = jnp.concatenate([emb[i * 16:(i + 1) * 16] for i in range(3)], axis=1)
        for r in range(1, NZ):
            e3_copy(r).start()

    def advantage():
        for r in range(1, CLIPS):
            c = lax.rem(clip + r, CLIPS)
            rcopy(rsb, rrb.at[c], r_s.at[r - 1], r_r.at[c], (c, seq)).wait_recv()
        total = rrb[0]
        for c in range(1, CLIPS):
            total = total + rrb[c]
        adv = rrb[clip] - total / CLIPS
        advb[...] = adv
        adv1 = adv[0:1, 0:1]
        ld_small[7].wait()
        gadv[...] = gate_ref[...] * adv1

    def e_first():
        def tile(j, carry):
            cols = pl.ds(pl.multiple_of(j * TILE, TILE), TILE)
            g = jnp.dot(samp[...], cot2[pl.ds(0, TOK), cols], preferred_element_type=F32)
            e_own[:, cols] = g
            eo[:, cols] = g.astype(BF16)
            return carry
        lax.fori_loop(0, D // TILE, tile, 0)
        e1_copy().start()

    def e1_copy():
        rows = pl.ds(pl.multiple_of(oc * 32, 32), 32)
        return rcopy(eo.at[rows], er, e1_s, e1_r, core_dev)

    def e_sum():
        e1_copy().wait_recv()
        es[...] = e_own[pl.ds(pl.multiple_of(core * 32, 32), 32), :] + er[...].astype(F32)

    def dot_cols(*pieces):
        parts = [cot2[:, a:a + w] for a, w in pieces]
        rhs = parts[0] if len(parts) == 1 else jnp.concatenate(parts, axis=1)
        return jnp.dot(a2[...], rhs, preferred_element_type=F32)

    def g_chunk(k):
        gs[k, :, :2 * THIRD] = dot_cols(((2 * k + 1) * SL, 2 * THIRD))
        gs[k, :, 2 * THIRD:] = dot_cols((2 * k * SL, THIRD))

    def g_side():
        for m in range(2):
            o = m * 2 * ZW
            j = 4 * m
            gside[:, o:o + 2 * THIRD] = dot_cols((j * SL + THIRD, 2 * THIRD))
            gside[:, o + 2 * THIRD:o + 4 * THIRD] = dot_cols(
                ((j + 1) * SL + 2 * THIRD, THIRD), ((j + 3) * SL + 2 * THIRD, THIRD)
            )
            gside[:, o + 4 * THIRD:o + 6 * THIRD] = dot_cols(((j + 2) * SL + THIRD, 2 * THIRD))

    def f_copy(q):
        to = (q // 2, z * 4 + (q % 2) * 2 + core)
        w = pl.ds(0, mwidth(q // 2))
        return rcopy(fs.at[q, :, w], fr.at[me16, :, w], f_s.at[q], f_r.at[me16], to)

    def final(k):
        zlong(3, k).wait_recv()
        zshort(2, k).wait_recv()
        both = gs[k, zrows(z), :] + zlr[3, k].astype(F32) + zsr[2, k].astype(F32)
        for j in range(2):
            jj = 2 * k + j
            w = mwidth(jj)
            r = both[:, :w] if j else both[:, 2 * THIRD:]
            r = r * gadv[:, jj * SL:jj * SL + w]
            for l in range(2):
                q = (2 * k + j) * 2 + l
                fs[q, :, :w] = r[l * ROWS:(l + 1) * ROWS].astype(BF16)

                @pl.when(me16 != q)
                def _():
                    f_copy(q).start()

    def w_use(slot, first=False, own=False):
        if own:
            ld_w.wait()
        else:
            w_core_other(slot, 0).wait_recv()
            w_core_other(slot, 1).wait_recv()
        cols = pl.ds(pl.multiple_of(slot * SL, SL), SL)
        proj = jnp.dot(vals_v[...], wf[slot], preferred_element_type=F32)
        emb = jnp.dot(samp_t[...], ew_ref[:, cols], preferred_element_type=F32)
        bo_ref[:, cols] = (emb + gate_ref[:, cols] * proj).astype(BF16)
        br = branch[:, cols]
        for i in range(2):
            g = lax.dot_general(br, wf[slot, i * HALF:(i + 1) * HALF], (((1,), (1,)), ((), ())), preferred_element_type=F32)
            if first:
                ga_acc[:, i * HALF:(i + 1) * HALF] = g
            else:
                ga_acc[:, i * HALF:(i + 1) * HALF] += g

    def e_four():
        for r in range(1, NZ):
            o = zr(r)
            rcopy(ef.at[me4, o], ef.at[me4, o], e3_s.at[r - 1], e3_r.at[o], dev(x, h, lo, o, core)).wait_recv()
        for i in range(3):
            e4_copy(i).start()

    def e_five():
        for i, q in enumerate((core * 2 + olo, oc * 2 + lo, oc * 2 + olo)):
            rcopy(ef.at[q], ef.at[q], e4_s.at[i], e4_r.at[q], side).wait_recv()
        for q in range(4):
            for d in range(NZ):
                ge_ref[q * 16:(q + 1) * 16, d * SL:(d + 1) * SL] = ef[q, d].astype(F32) * advb[0:1, 0:1]
        pltpu.make_async_copy(ge_ref, ge_out, loc.at[4]).start()

    def stage_1():
        got(a_slot(1), 0)
        got(a_slot(3), 0)
        w_fwd(h * NX + xr(-sgn), 0, wx_s.at[4], xs).start()
        w_fwd(a_slot(1), 0, wy_s.at[2], cross).start()
        w_fwd(a_slot(3), 0, wy_s.at[3], cross).start()

    def stage_2():
        got(a_slot(1), 1)
        got(a_slot(3), 1)
        w_fwd(h * NX + xr(-sgn), 1, wx_s.at[5], xs).start()

    def stage_2b():
        got(b_slot(0), 0)
        got(b_slot(0), 1)
        w_fwd(b_slot(0), 1, wx_s.at[6], xp).start()
        w_fwd(b_slot(0), 1, wx_s.at[7], xm).start()

    def stage_3():
        got(a_slot(2), 0)
        w_fwd(a_slot(2), 0, wy_s.at[4], cross).start()

    def stage_4():
        got(a_slot(2), 1)

    def stage_5(i):
        got(b_slot(i), 0)

    def stage_6():
        got(b_slot(1), 1)
        got(b_slot(3), 1)
        w_fwd(oh * NX + xr(-sgn), 1, wx_s.at[8], xs).start()

    def stage_8():
        got(b_slot(2), 1)

    e_first()
    cp_a2.wait_recv()
    cp_cot[0].wait_recv()
    g_chunk(0)
    zstep(0, 0)
    for k in range(1, NC):
        cp_cot[k].wait_recv()
    g_side()
    e_sum()
    side_send()
    for k in range(1, NC):
        g_chunk(k)
        zstep(0, k)
    zstep(1, 0)
    advantage()
    stage_1()
    ld_small[6].wait()
    scaled = (cot2[pl.ds(0, TOK), :].astype(F32) * advb[0:1, 0:1]).astype(BF16)
    branch[...] = (scaled.astype(F32) * gate_ref[...]).astype(BF16)
    zstep(1, 1)
    sstep(0)
    stage_2b()
    stage_2()
    w_use(clip, first=True, own=True)
    zstep(2, 0)
    zstep(1, 3)
    w_use(a_slot(3))
    zstep(1, 2)
    sstep(1)
    w_use(b_slot(0))
    zstep(3, 0)
    w_use(a_slot(1))
    stage_3()
    stage_5(1)
    stage_4()
    stage_5(3)
    stage_6()
    zstep(2, 2)
    zstep(2, 1)
    sstep(2)
    final(0)
    w_use(b_slot(1))
    zstep(2, 3)
    w_use(a_slot(2))
    stage_5(2)
    sstep(3)
    zstep(3, 2)
    stage_8()
    zstep(3, 1)
    w_use(b_slot(3))
    zstep(3, 3)
    sfinal()
    final(2)
    final(1)
    final(3)
    w_use(b_slot(2))
    pltpu.make_async_copy(bo_ref, bo_out, loc.at[6]).start()
    ga_ref[...] = ga_acc[...].astype(BF16)
    pltpu.make_async_copy(ga_ref, ga_out, loc.at[7]).start()
    e_four()
    e_five()

    fr[me16] = fs[me16]
    frs[clip] = fss[clip]
    for par in range(2):
        @pl.when(lax.rem(clip, 2) == par)
        def _():
            wm, ws = pl.ds(0, mwidth(par)), pl.ds(0, swidth(par))
            for q in range(16):
                @pl.when(me16 != q)
                def _():
                    rcopy(fs.at[q, :, wm], fr.at[q, :, wm], f_s.at[q], f_r.at[q], core_dev).wait_recv()
            for j in range(CLIPS):
                @pl.when(clip != j)
                def _():
                    rcopy(fss.at[j, :, ws], frs.at[j, :, ws], f2_s.at[j], f2_r.at[j], core_dev).wait_recv()
            acc = fr[0, :, wm].astype(F32)
            for q in range(1, 16):
                acc = acc + fr[q, :, wm].astype(F32)
            gw_ref[:, :mwidth(par)] = acc
            acc = frs[0, :, ws].astype(F32)
            for j in range(1, CLIPS):
                acc = acc + frs[j, :, ws].astype(F32)
            gw_ref[:, mwidth(par):] = acc
    pltpu.make_async_copy(gw_ref, gw_out, loc.at[5]).start()

    pltpu.make_async_copy(ge_ref, ge_out, loc.at[4]).wait()
    pltpu.make_async_copy(gw_ref, gw_out, loc.at[5]).wait()
    pltpu.make_async_copy(bo_ref, bo_out, loc.at[6]).wait()
    pltpu.make_async_copy(ga_ref, ga_out, loc.at[7]).wait()
    for cp in rsends:
        cp.wait_send()
    for cp in cp_cot:
        cp.wait_send()
    cp_a2.wait_send()
    for n in range(9):
        w_fwd(a_slot(1), 0, wx_s.at[n], xp).wait_send()
    for n in range(5):
        w_fwd(a_slot(1), 0, wy_s.at[n], side).wait_send()
    for i in range(2):
        for n in range(1, 4):
            w_core(a_slot(n), i).wait_send()
        for n in range(4):
            w_core(b_slot(n), i).wait_send()
    for i in range(NZ):
        side_copy(i).wait_send()
    for t in range(4):
        slong(t).wait_send()
        if t < 3:
            sshort(t).wait_send()
        for k in range(NC):
            zlong(t, k).wait_send()
            if t < 3:
                zshort(t, k).wait_send()
    for q in range(16):
        @pl.when(me16 != q)
        def _():
            f_copy(q).wait_send()
    for j in range(CLIPS):
        @pl.when(clip != j)
        def _():
            fs_copy(j).wait_send()
    e1_copy().wait_send()
    for r in range(1, NZ):
        e3_copy(r).wait_send()
    for i in range(3):
        e4_copy(i).wait_send()


def fused(step, rewards, lat, noi, vc, vu, ew, gate, vals, w, cot):
    anyspace = pl.BlockSpec(memory_space=pl.ANY)
    dma = pltpu.SemaphoreType.DMA
    scratch = [
        pltpu.SMEM((1,), jnp.int32),
        pltpu.SMEM((1,), F32),
        pltpu.VMEM((CH, TOK), F32),
        pltpu.VMEM((CH, TOK), F32),
        pltpu.VMEM((CH, TOK), BF16),
        pltpu.VMEM((CH, TOK), BF16),
        pltpu.VMEM((CH, D), BF16),
        pltpu.VMEM((1, D), F32),
        pltpu.VMEM((TOK, H), BF16),
        pltpu.VMEM((2 * TOK, D), BF16),
        pltpu.VMEM((HALF, 2 * TOK), BF16),
        pltpu.VMEM((2, HALF, TOK), BF16),
        pltpu.VMEM((CLIPS, H, SL), BF16),
        pltpu.VMEM((NC, HALF, ZW), F32),
        pltpu.VMEM((32, D), F32),
        pltpu.VMEM((4, NC, ZROWS, ZW), BF16),
        pltpu.VMEM((4, NC, ZROWS, ZW), BF16),
        pltpu.VMEM((3, NC, ZROWS, ZW), BF16),
        pltpu.VMEM((3, NC, ZROWS, ZW), BF16),
        pltpu.VMEM((16, ROWS, 2 * THIRD), BF16),
        pltpu.VMEM((16, ROWS, 2 * THIRD), BF16),
        pltpu.VMEM((CLIPS, ROWS, 2 * THIRD), BF16),
        pltpu.VMEM((CLIPS, ROWS, 2 * THIRD), BF16),
        pltpu.VMEM((4, NZ, 16, SL), BF16),
        pltpu.VMEM((NZ, ROWS, SW), BF16),
        pltpu.VMEM((NZ, ROWS, SW), BF16),
        pltpu.VMEM((4, ROWS, SW), BF16),
        pltpu.VMEM((4, ROWS, SW), BF16),
        pltpu.VMEM((3, ROWS, SW), BF16),
        pltpu.VMEM((3, ROWS, SW), BF16),
        pltpu.VMEM((CH, D), F32),
        pltpu.VMEM((CH, D), BF16),
        pltpu.VMEM((32, D), BF16),
        pltpu.VMEM((HALF, NC * ZW), F32),
        pltpu.VMEM((8, 128), F32),
        pltpu.VMEM((CLIPS, 8, 128), F32),
        pltpu.VMEM((CH, TOK), BF16),
        pltpu.VMEM((TOK, CH), BF16),
        pltpu.VMEM((TOK, D), BF16),
        pltpu.VMEM((1, D), F32),
        pltpu.VMEM((8, 128), F32),
        pltpu.VMEM((TOK, H), F32),
        pltpu.VMEM((TOK, D), BF16),
        pltpu.VMEM((TOK, H), BF16),
        pltpu.VMEM((ROWS, SL), F32),
        pltpu.VMEM((CH, D), F32),
        dma((16,)), dma((7,)), dma((8,)), dma((NC,)), dma((NC,)), dma, dma,
        dma((9,)), dma((5,)), dma((16,)), dma((16,)), dma((16,)),
        dma((NZ,)), dma((NZ,)), dma((4,)), dma((4,)), dma((3,)), dma((3,)),
        dma((4 * NC,)), dma((4 * NC,)), dma((3 * NC,)), dma((3 * NC,)),
        dma((16,)), dma((16,)), dma((8,)), dma((8,)), dma, dma, dma((7,)), dma((8,)), dma((3,)), dma((4,)),
    ]
    return pl.pallas_call(
        kernel,
        name="fused_step",
        out_shape=(
            jax.ShapeDtypeStruct((TOK, D), BF16),
            jax.ShapeDtypeStruct((TOK, H), BF16),
            jax.ShapeDtypeStruct((ROWS, SL), F32),
            jax.ShapeDtypeStruct((CH, D), F32),
        ),
        in_specs=[anyspace] * 11,
        out_specs=(anyspace, anyspace, anyspace, anyspace),
        scratch_shapes=scratch,
        compiler_params=pltpu.CompilerParams(
            collective_id=0, has_side_effects=True, vmem_limit_bytes=58 * 2**20
        ),
    )(step, rewards, lat, noi, vc, vu, ew, gate, vals, w, cot)


def copy_kernel(bo, ga, gw, ge, bo_o, ga_o, gw_o, ge_o, v0, v1, v2, v3, ins, outs):
    loads, stores = [], []
    n = 0
    for src, mid, dst, parts in ((bo, v0, bo_o, 4), (ga, v1, ga_o, 2), (ge, v3, ge_o, 2), (gw, v2, gw_o, 1)):
        rows = src.shape[0] // parts
        for p in range(parts):
            at = pl.ds(p * rows, rows)
            loads.append(pltpu.make_async_copy(src.at[at], mid.at[at], ins.at[n]))
            stores.append(pltpu.make_async_copy(mid.at[at], dst.at[at], outs.at[n]))
            n += 1
    for c in loads:
        c.start()
    for a, b in zip(loads, stores):
        a.wait()
        b.start()
    for c in stores:
        c.wait()


def copied(*arrays):
    anyspace = pl.BlockSpec(memory_space=pl.ANY)
    return pl.pallas_call(
        copy_kernel,
        name="results",
        out_shape=tuple(jax.ShapeDtypeStruct(a.shape, a.dtype) for a in arrays),
        in_specs=[anyspace] * 4,
        out_specs=(anyspace,) * 4,
        scratch_shapes=[pltpu.VMEM(a.shape, a.dtype) for a in arrays]
        + [pltpu.SemaphoreType.DMA((9,)), pltpu.SemaphoreType.DMA((9,))],
        compiler_params=pltpu.CompilerParams(vmem_limit_bytes=60 * 2**20),
    )(*arrays)


def local(latent, sample_noise, vel_cond, vel_uncond, step_index, embed_w, gate_scale, attn_vals, out_w, cotangent, rewards):
    bo, ga, gw, ge = copied(*fused(
        step_index, rewards, latent[0], sample_noise[0], vel_cond[0], vel_uncond[0], embed_w,
        gate_scale, attn_vals[0], out_w, cotangent[0],
    ))
    return bo[None], ga[None], gw, ge[None]


def solution(mesh):
    in_specs = (
        P("clip", None, "seq"),
        P("clip", None, "seq"),
        P("clip", None, "seq"),
        P("clip", None, "seq"),
        P(),
        P(),
        P("clip", None),
        P("clip", "seq", None),
        P(None, "clip"),
        P("clip", "seq", None),
        P("clip"),
    )
    out_specs = (
        P("clip", "seq", None),
        P("clip", "seq", None),
        P("seq", "clip"),
        P("clip", None, None),
    )
    return jax.shard_map(local, mesh=mesh, in_specs=in_specs, out_specs=out_specs, check_vma=False)
```

```python
import jax
import jax.numpy as jnp
from jax import lax
from jax.experimental import pallas as pl
from jax.experimental.pallas import tpu as pltpu
from jax.sharding import PartitionSpec as P

NSTEPS = 16
SHIFT_FACTOR = 7.0
GUIDANCE = 6.0
NOISE_LEVEL = 0.3

D = 3072
H = 1536
CH = 64
TOK = 256
NX, NZ = 4, 8
CLIPS = 8
SL = D // CLIPS
HALF = H // 2
ROWS = 48
ZROWS = 2 * ROWS
NC = 4
CC = D // NC
TILE = 256
QR = H // 4
THIRD = SL // 3
ZW = 3 * THIRD
SW = NC * ZW

MESH = pl.DeviceIdType.MESH


def mwidth(j):
    return 2 * THIRD if j % 2 else THIRD


def swidth(j):
    return SL - mwidth(j)


def soffset(j):
    return (j // 4) * 2 * ZW + (0, 2 * THIRD, 4 * THIRD, 3 * THIRD)[j % 4]

F32, BF16 = jnp.float32, jnp.bfloat16


def sigma_level(index):
    tval = 1.0 - index.astype(F32) / NSTEPS
    return SHIFT_FACTOR * tval / (1.0 + (SHIFT_FACTOR - 1.0) * tval)


def dev(x, h, lo, z, core):
    return (h * NX + x, z * 4 + lo * 2 + core)


def kernel(
    step_in, rew_in, lat_in, noi_in, vc_in, vu_in, ew_in, gate_in, vals_ref, w_ref, cot_ref,
    bo_out, ga_out, gw_out, ge_out,
    step_ref, rew_ref, lat_ref, noi_ref, vc_ref, vu_ref, ew_ref, gate_ref, vals_v, cot2, a2, vts, wf, gs, es, zls, zlr, zss, zsr, fs, fr, fss, frs, ef, ehs, ehr, e2s, e2r,
    sss, ssr, szls, szlr, szss, szsr,
    e_own, eo, er, gside, rsb, rrb, samp, samp_t, branch, gadv, advb, ga_acc, bo_ref, ga_ref, gw_ref, ge_ref,
    loc, r_s, r_r, cot_s, cot_r, a2_s, a2_r, wx_s, wy_s, wc_s, w_r, wc_r,
    ss_s, ss_r, szl_s, szl_r, szs_s, szs_r, zl_s, zl_r, zs_s, zs_r, f_s, f_r, f2_s, f2_r, bo_s, e1_s, e1_r, eh_s, eh_r, e2_s, e2_r, e3_s, e3_r, e4_s, e4_r,
):
    clip = lax.axis_index("clip")
    seq = lax.axis_index("seq")
    h, x = lax.div(clip, NX), lax.rem(clip, NX)
    z, lo, core = lax.div(seq, 4), lax.rem(lax.div(seq, 2), 2), lax.rem(seq, 2)
    oc, olo, oh = 1 - core, 1 - lo, 1 - h
    sgn = 1 - 2 * core

    def xr(n):
        return lax.rem(x + n + NX, NX)

    def zr(n):
        return lax.rem(z + n + NZ, NZ)

    def rcopy(src, dst, ss, rs, to):
        return pltpu.make_async_remote_copy(
            src_ref=src, dst_ref=dst, send_sem=ss, recv_sem=rs, device_id=to, device_id_type=MESH
        )

    bar = pltpu.get_barrier_semaphore()
    me16 = clip * 2 + lo
    partners = []
    for r in range(1, 16):
        o = lax.rem(me16 + r, 16)
        oclip, olo_ = lax.div(o, 2), lax.rem(o, 2)
        partners.append((oclip, z * 4 + olo_ * 2 + core))
    for r in range(1, NZ):
        partners.append(dev(x, h, lo, zr(r), core))
    partners.append(dev(x, h, lo, z, oc))
    partners.append(dev(x, h, olo, z, oc))
    for p in partners:
        pl.semaphore_signal(bar, inc=1, device_id=p, device_id_type=MESH)

    ld_vals = pltpu.make_async_copy(vals_ref, vals_v, loc.at[0])
    ld_cot = pltpu.make_async_copy(cot_ref, cot2.at[pl.ds(0, TOK)], loc.at[1])
    ld_w = pltpu.make_async_copy(w_ref, wf.at[clip], loc.at[2])
    ld_vals.start()
    ld_cot.start()
    ld_w.start()
    small = ((step_in, step_ref), (rew_in, rew_ref), (lat_in, lat_ref), (noi_in, noi_ref),
             (vc_in, vc_ref), (vu_in, vu_ref), (ew_in, ew_ref), (gate_in, gate_ref))
    ld_small = [pltpu.make_async_copy(a, b, loc.at[8 + i]) for i, (a, b) in enumerate(small)]
    for cp in ld_small:
        cp.start()

    for cp in ld_small[:6]:
        cp.wait()
    rsb[...] = jnp.full((8, 128), rew_ref[0], F32)
    rrb[clip] = jnp.full((8, 128), rew_ref[0], F32)
    idx = jnp.full((1, TOK), step_ref[0], jnp.int32)
    sig_now = sigma_level(idx)
    sig_next = sigma_level(idx + 1)
    uncond = vu_ref[...].astype(F32)
    guided = uncond + GUIDANCE * (vc_ref[...].astype(F32) - uncond)
    spread = NOISE_LEVEL * jnp.sqrt(sig_now - sig_next)
    sampled = lat_ref[...] + (sig_next - sig_now) * guided + spread * noi_ref[...]
    samp_t[...] = sampled.T.astype(BF16)
    samp_b = sampled.astype(BF16)
    samp[...] = samp_b

    ld_vals.wait()
    for b in range(H // 384):
        vt = vals_v[:, b * 384:(b + 1) * 384].T
        for q in range(8):
            s = b * 8 + q
            zz, ll, cc = s // 4, (s // 2) % 2, s % 2
            vts[cc, pl.ds(zz * ZROWS + ll * ROWS, ROWS), :] = vt[q * ROWS:(q + 1) * ROWS]
    a2[:, pl.ds(0, TOK)] = vts[core]

    pl.semaphore_wait(bar, len(partners))

    core_dev = dev(x, h, lo, z, oc)
    cp_a2 = rcopy(vts.at[oc], a2.at[:, pl.ds(TOK, TOK)], a2_s, a2_r, core_dev)
    cp_a2.start()
    cp_cot = []
    for k in range(NC):
        cols = pl.ds(k * CC, CC)
        cp = rcopy(cot_ref.at[:, cols], cot2.at[pl.ds(TOK, TOK), cols], cot_s.at[k], cot_r.at[k], core_dev)
        cp.start()
        cp_cot.append(cp)
    rsends = []
    for r in range(1, CLIPS):
        c = lax.rem(clip + r, CLIPS)
        cp = rcopy(rsb, rrb.at[clip], r_s.at[r - 1], r_r.at[clip], (c, seq))
        cp.start()
        rsends.append(cp)

    side = dev(x, h, olo, z, core)
    cross = dev(x, oh, olo, z, core)

    def quarter(i):
        return pl.ds(pl.multiple_of((core * 2 + i) * QR, QR), QR)

    def w_own(i, ss, to):
        return rcopy(w_ref.at[quarter(i)], wf.at[clip, quarter(i)], ss, w_r.at[clip * 2 + i], to)

    def w_fwd(slot, i, ss, to):
        return rcopy(wf.at[slot, quarter(i)], wf.at[slot, quarter(i)], ss, w_r.at[slot * 2 + i], to)

    xp = dev(xr(1), h, lo, z, core)
    xm = dev(xr(-1), h, lo, z, core)
    xs = dev(xr(sgn), h, lo, z, core)
    for i in range(2):
        w_own(i, wx_s.at[2 * i], xp).start()
        w_own(i, wx_s.at[2 * i + 1], xm).start()
        w_own(i, wy_s.at[i], cross).start()

    def a_slot(i):
        return h * NX + xr(i)

    def b_slot(i):
        return oh * NX + xr(i)

    def w_core(slot, i):
        n = slot * 2 + i
        return rcopy(wf.at[slot, quarter(i)], wf.at[slot, quarter(i)], wc_s.at[n], wc_r.at[n], core_dev)

    def w_core_other(slot, i):
        n = slot * 2 + i
        rows = pl.ds(pl.multiple_of((oc * 2 + i) * QR, QR), QR)
        return rcopy(wf.at[slot, rows], wf.at[slot, rows], wc_s.at[n], wc_r.at[n], core_dev)

    def got(slot, i):
        w_fwd(slot, i, wx_s.at[0], xp).wait_recv()
        w_core(slot, i).start()

    ld_cot.wait()

    zl_dev = dev(x, h, lo, zr(sgn), core)
    zs_dev = dev(x, h, lo, zr(-sgn), core)

    def zlong(t, k):
        n = t * NC + k
        return rcopy(zls.at[t, k], zlr.at[t, k], zl_s.at[n], zl_r.at[n], zl_dev)

    def zshort(t, k):
        n = t * NC + k
        return rcopy(zss.at[t, k], zsr.at[t, k], zs_s.at[n], zs_r.at[n], zs_dev)

    def zrows(d):
        return pl.ds(pl.multiple_of(d * ZROWS, ZROWS), ZROWS)

    def zadd(t, k, d, out, got_ref):
        v = gs[k, zrows(d), :]
        if t:
            v = v + got_ref[t - 1, k].astype(F32)
        out[t, k] = v.astype(BF16)

    def zstep(t, k):
        if t:
            zlong(t - 1, k).wait_recv()
        zadd(t, k, zr(sgn * (4 - t)), zls, zlr)
        zlong(t, k).start()
        if t < 3:
            if t:
                zshort(t - 1, k).wait_recv()
            zadd(t, k, zr(-sgn * (3 - t)), zss, zsr)
            zshort(t, k).start()

    def lrows(d, l):
        return pl.ds(pl.multiple_of(d * ZROWS + l * ROWS, ROWS), ROWS)

    def sown(d, l):
        return gside[lrows(d, l), :]

    sorder = (sgn * 4, -sgn * 3, sgn * 3, -sgn * 2, sgn * 2, -sgn, sgn, 0)

    me4 = core * 2 + lo

    def e3_copy(r):
        return rcopy(ef.at[me4, z], ef.at[me4, z], e3_s.at[r - 1], e3_r.at[z], dev(x, h, lo, zr(r), core))

    def e4_copy(i):
        to = [side, core_dev, dev(x, h, olo, z, oc)][i]
        return rcopy(ef.at[me4], ef.at[me4], e4_s.at[i], e4_r.at[me4], to)

    def fs_copy(j):
        w = pl.ds(0, swidth(j))
        return rcopy(fss.at[j, :, w], frs.at[clip, :, w], f2_s.at[j], f2_r.at[clip], (j, seq))

    def side_copy(i):
        return rcopy(sss.at[i], ssr.at[i], ss_s.at[i], ss_r.at[i], side)

    def side_send(first, end):
        for i in range(first, end):
            sss[i] = sown(zr(sorder[i]), olo).astype(BF16)
            side_copy(i).start()

    def slong(t):
        return rcopy(szls.at[t], szlr.at[t], szl_s.at[t], szl_r.at[t], zl_dev)

    def sshort(t):
        return rcopy(szss.at[t], szsr.at[t], szs_s.at[t], szs_r.at[t], zs_dev)

    def splong(t):
        side_copy(2 * t).wait_recv()
        v = sown(zr(sgn * (4 - t)), lo) + ssr[2 * t].astype(F32)
        if t:
            slong(t - 1).wait_recv()
            v = v + szlr[t - 1].astype(F32)
        szls[t] = v.astype(BF16)
        slong(t).start()

    def spshort(t):
        side_copy(2 * t + 1).wait_recv()
        v = sown(zr(-sgn * (3 - t)), lo) + ssr[2 * t + 1].astype(F32)
        if t:
            sshort(t - 1).wait_recv()
            v = v + szsr[t - 1].astype(F32)
        szss[t] = v.astype(BF16)
        sshort(t).start()

    def sfinal():
        side_copy(7).wait_recv()
        slong(3).wait_recv()
        sshort(2).wait_recv()
        v = sown(z, lo) + ssr[7].astype(F32) + szlr[3].astype(F32) + szsr[2].astype(F32)
        for j in range(CLIPS):
            o, w, c = j * SL + mwidth(j), swidth(j), soffset(j)
            fss[j, :, :w] = (v[:, c:c + w] * gadv[:, o:o + w]).astype(BF16)

            @pl.when(clip != j)
            def _():
                fs_copy(j).start()

    def eh_copy():
        return rcopy(ehs, ehr, eh_s, eh_r, side)

    def e2_copy(r):
        return rcopy(e2s.at[zr(r)], e2r.at[z], e2_s.at[r - 1], e2_r.at[z], dev(x, h, lo, zr(r), core))

    def e_two():
        eh_copy().wait_recv()
        part = es[pl.ds(pl.multiple_of(lo * 16, 16), 16), :] + ehr[...].astype(F32)
        for d in range(NZ):
            e2s[d] = part[:, d * SL:(d + 1) * SL].astype(BF16)
        for r in range(1, NZ):
            e2_copy(r).start()
        e2r[z] = e2s[z]

    def e_three():
        for r in range(1, NZ):
            o = zr(r)
            rcopy(e2s.at[o], e2r.at[o], e2_s.at[r - 1], e2_r.at[o], dev(x, h, lo, o, core)).wait_recv()
        tot = e2r[0].astype(F32)
        for d in range(1, NZ):
            tot = tot + e2r[d].astype(F32)
        ef[me4, z] = tot.astype(BF16)
        for r in range(1, NZ):
            e3_copy(r).start()

    def advantage():
        for r in range(1, CLIPS):
            c = lax.rem(clip + r, CLIPS)
            rcopy(rsb, rrb.at[c], r_s.at[r - 1], r_r.at[c], (c, seq)).wait_recv()
        total = rrb[0]
        for c in range(1, CLIPS):
            total = total + rrb[c]
        adv = rrb[clip] - total / CLIPS
        advb[...] = adv
        adv1 = adv[0:1, 0:1]
        ld_small[7].wait()
        gadv[...] = gate_ref[...] * adv1

    def e_first():
        def tile(j, carry):
            cols = pl.ds(pl.multiple_of(j * TILE, TILE), TILE)
            g = jnp.dot(samp[...], cot2[pl.ds(0, TOK), cols], preferred_element_type=F32)
            e_own[:, cols] = g
            eo[:, cols] = g.astype(BF16)
            return carry
        lax.fori_loop(0, D // TILE, tile, 0)
        e1_copy().start()

    def e1_copy():
        rows = pl.ds(pl.multiple_of(oc * 32, 32), 32)
        return rcopy(eo.at[rows], er, e1_s, e1_r, core_dev)

    def e_sum():
        e1_copy().wait_recv()
        es[...] = e_own[pl.ds(pl.multiple_of(core * 32, 32), 32), :] + er[...].astype(F32)
        ehs[...] = es[pl.ds(pl.multiple_of(olo * 16, 16), 16), :].astype(BF16)
        eh_copy().start()

    def dot_cols(*pieces):
        parts = [cot2[:, a:a + w] for a, w in pieces]
        rhs = parts[0] if len(parts) == 1 else jnp.concatenate(parts, axis=1)
        return jnp.dot(a2[...], rhs, preferred_element_type=F32)

    def g_chunk(k):
        gs[k, :, :2 * THIRD] = dot_cols(((2 * k + 1) * SL, 2 * THIRD))
        gs[k, :, 2 * THIRD:] = dot_cols((2 * k * SL, THIRD))

    def g_side():
        for m in range(2):
            o = m * 2 * ZW
            j = 4 * m
            gside[:, o:o + 2 * THIRD] = dot_cols((j * SL + THIRD, 2 * THIRD))
            gside[:, o + 2 * THIRD:o + 4 * THIRD] = dot_cols(
                ((j + 1) * SL + 2 * THIRD, THIRD), ((j + 3) * SL + 2 * THIRD, THIRD)
            )
            gside[:, o + 4 * THIRD:o + 6 * THIRD] = dot_cols(((j + 2) * SL + THIRD, 2 * THIRD))

    def f_copy(q):
        to = (q // 2, z * 4 + (q % 2) * 2 + core)
        w = pl.ds(0, mwidth(q // 2))
        return rcopy(fs.at[q, :, w], fr.at[me16, :, w], f_s.at[q], f_r.at[me16], to)

    def final(k):
        zlong(3, k).wait_recv()
        zshort(2, k).wait_recv()
        both = gs[k, zrows(z), :] + zlr[3, k].astype(F32) + zsr[2, k].astype(F32)
        for j in range(2):
            jj = 2 * k + j
            w = mwidth(jj)
            r = both[:, :w] if j else both[:, 2 * THIRD:]
            r = r * gadv[:, jj * SL:jj * SL + w]
            for l in range(2):
                q = (2 * k + j) * 2 + l
                fs[q, :, :w] = r[l * ROWS:(l + 1) * ROWS].astype(BF16)

                @pl.when(me16 != q)
                def _():
                    f_copy(q).start()

    def bo_copy(slot):
        cols = pl.ds(pl.multiple_of(slot * SL, SL), SL)
        return pltpu.make_async_copy(bo_ref.at[:, cols], bo_out.at[:, cols], bo_s.at[slot])

    def w_use(slot, first=False, own=False, last=False):
        if own:
            ld_w.wait()
        else:
            w_core_other(slot, 0).wait_recv()
            w_core_other(slot, 1).wait_recv()
        cols = pl.ds(pl.multiple_of(slot * SL, SL), SL)
        proj = jnp.dot(vals_v[...], wf[slot], preferred_element_type=F32)
        emb = jnp.dot(samp_t[...], ew_ref[:, cols], preferred_element_type=F32)
        bo_ref[:, cols] = (emb + gate_ref[:, cols] * proj).astype(BF16)
        br = branch[:, cols]
        bo_copy(slot).start()
        for i in range(2):
            half = slice(i * HALF, (i + 1) * HALF)
            g = lax.dot_general(br, wf[slot, half], (((1,), (1,)), ((), ())), preferred_element_type=F32)
            if first:
                ga_acc[:, half] = g
            elif last:
                ga_ref[:, half] = (ga_acc[:, half] + g).astype(BF16)
            else:
                ga_acc[:, half] += g

    def e_four():
        for r in range(1, NZ):
            o = zr(r)
            rcopy(ef.at[me4, o], ef.at[me4, o], e3_s.at[r - 1], e3_r.at[o], dev(x, h, lo, o, core)).wait_recv()
        for i in range(3):
            e4_copy(i).start()

    def e_five():
        for i, q in enumerate((core * 2 + olo, oc * 2 + lo, oc * 2 + olo)):
            rcopy(ef.at[q], ef.at[q], e4_s.at[i], e4_r.at[q], side).wait_recv()
        for q in range(4):
            for d in range(NZ):
                ge_ref[q * 16:(q + 1) * 16, d * SL:(d + 1) * SL] = ef[q, d].astype(F32) * advb[0:1, 0:1]
        pltpu.make_async_copy(ge_ref, ge_out, loc.at[4]).start()

    def stage_1():
        got(a_slot(1), 0)
        got(a_slot(3), 0)
        w_fwd(h * NX + xr(-sgn), 0, wx_s.at[4], xs).start()
        w_fwd(a_slot(1), 0, wy_s.at[2], cross).start()
        w_fwd(a_slot(3), 0, wy_s.at[3], cross).start()

    def stage_2():
        got(a_slot(1), 1)
        got(a_slot(3), 1)
        w_fwd(h * NX + xr(-sgn), 1, wx_s.at[5], xs).start()

    def stage_2b():
        got(b_slot(0), 0)
        got(b_slot(0), 1)
        w_fwd(b_slot(0), 1, wx_s.at[6], xp).start()
        w_fwd(b_slot(0), 1, wx_s.at[7], xm).start()

    def stage_3():
        got(a_slot(2), 0)
        w_fwd(a_slot(2), 0, wy_s.at[4], cross).start()

    def stage_4():
        got(a_slot(2), 1)

    def stage_5(i):
        got(b_slot(i), 0)

    def stage_6():
        got(b_slot(1), 1)
        got(b_slot(3), 1)
        w_fwd(oh * NX + xr(-sgn), 1, wx_s.at[8], xs).start()

    def stage_8():
        got(b_slot(2), 1)

    e_first()
    cp_a2.wait_recv()
    cp_cot[0].wait_recv()
    g_chunk(0)
    zstep(0, 0)
    cp_cot[2].wait_recv()
    g_chunk(2)
    zstep(0, 2)
    cp_cot[1].wait_recv()
    cp_cot[3].wait_recv()
    g_side()
    side_send(0, 2)
    e_sum()
    side_send(2, 8)
    g_chunk(1)
    zstep(0, 1)
    g_chunk(3)
    zstep(0, 3)
    stage_1()
    zstep(1, 2)
    advantage()
    zstep(1, 0)
    ld_small[6].wait()
    scaled = (cot2[pl.ds(0, TOK), :].astype(F32) * advb[0:1, 0:1]).astype(BF16)
    branch[...] = (scaled.astype(F32) * gate_ref[...]).astype(BF16)
    splong(0)
    zstep(1, 3)
    zstep(1, 1)
    stage_2b()
    e_two()
    zstep(2, 2)
    spshort(0)
    stage_2()
    zstep(2, 0)
    w_use(b_slot(0), first=True)
    splong(1)
    zstep(2, 3)
    stage_3()
    w_use(clip, own=True)
    zstep(2, 1)
    w_use(a_slot(1))
    stage_6()
    e_three()
    stage_5(1)
    spshort(1)
    zstep(3, 2)
    stage_5(3)
    w_use(a_slot(3))
    splong(2)
    stage_4()
    zstep(3, 0)
    zstep(3, 3)
    w_use(b_slot(1))
    zstep(3, 1)
    stage_8()
    spshort(2)
    stage_5(2)
    splong(3)
    e_four()
    final(2)
    final(3)
    final(0)
    final(1)
    w_use(b_slot(3))
    sfinal()
    w_use(b_slot(2))
    w_use(a_slot(2), last=True)
    pltpu.make_async_copy(ga_ref, ga_out, loc.at[7]).start()
    e_five()

    fr[me16] = fs[me16]
    frs[clip] = fss[clip]
    for par in range(2):
        @pl.when(lax.rem(clip, 2) == par)
        def _():
            wm, ws = pl.ds(0, mwidth(par)), pl.ds(0, swidth(par))
            for q in range(16):
                @pl.when(me16 != q)
                def _():
                    rcopy(fs.at[q, :, wm], fr.at[q, :, wm], f_s.at[q], f_r.at[q], core_dev).wait_recv()
            for j in range(CLIPS):
                @pl.when(clip != j)
                def _():
                    rcopy(fss.at[j, :, ws], frs.at[j, :, ws], f2_s.at[j], f2_r.at[j], core_dev).wait_recv()
            acc = fr[0, :, wm].astype(F32)
            for q in range(1, 16):
                acc = acc + fr[q, :, wm].astype(F32)
            gw_ref[:, :mwidth(par)] = acc
            acc = frs[0, :, ws].astype(F32)
            for j in range(1, CLIPS):
                acc = acc + frs[j, :, ws].astype(F32)
            gw_ref[:, mwidth(par):] = acc
    pltpu.make_async_copy(gw_ref, gw_out, loc.at[5]).start()

    pltpu.make_async_copy(ge_ref, ge_out, loc.at[4]).wait()
    pltpu.make_async_copy(gw_ref, gw_out, loc.at[5]).wait()
    for j in range(CLIPS):
        bo_copy(j).wait()
    pltpu.make_async_copy(ga_ref, ga_out, loc.at[7]).wait()
    for cp in rsends:
        cp.wait_send()
    for cp in cp_cot:
        cp.wait_send()
    cp_a2.wait_send()
    for n in range(9):
        w_fwd(a_slot(1), 0, wx_s.at[n], xp).wait_send()
    for n in range(5):
        w_fwd(a_slot(1), 0, wy_s.at[n], side).wait_send()
    for i in range(2):
        for n in range(1, 4):
            w_core(a_slot(n), i).wait_send()
        for n in range(4):
            w_core(b_slot(n), i).wait_send()
    for i in range(NZ):
        side_copy(i).wait_send()
    for t in range(4):
        slong(t).wait_send()
        if t < 3:
            sshort(t).wait_send()
        for k in range(NC):
            zlong(t, k).wait_send()
            if t < 3:
                zshort(t, k).wait_send()
    for q in range(16):
        @pl.when(me16 != q)
        def _():
            f_copy(q).wait_send()
    for j in range(CLIPS):
        @pl.when(clip != j)
        def _():
            fs_copy(j).wait_send()
    e1_copy().wait_send()
    eh_copy().wait_send()
    for r in range(1, NZ):
        e2_copy(r).wait_send()
        e3_copy(r).wait_send()
    for i in range(3):
        e4_copy(i).wait_send()


def fused(step, rewards, lat, noi, vc, vu, ew, gate, vals, w, cot):
    anyspace = pl.BlockSpec(memory_space=pl.ANY)
    dma = pltpu.SemaphoreType.DMA
    scratch = [
        pltpu.SMEM((1,), jnp.int32),
        pltpu.SMEM((1,), F32),
        pltpu.VMEM((CH, TOK), F32),
        pltpu.VMEM((CH, TOK), F32),
        pltpu.VMEM((CH, TOK), BF16),
        pltpu.VMEM((CH, TOK), BF16),
        pltpu.VMEM((CH, D), BF16),
        pltpu.VMEM((1, D), F32),
        pltpu.VMEM((TOK, H), BF16),
        pltpu.VMEM((2 * TOK, D), BF16),
        pltpu.VMEM((HALF, 2 * TOK), BF16),
        pltpu.VMEM((2, HALF, TOK), BF16),
        pltpu.VMEM((CLIPS, H, SL), BF16),
        pltpu.VMEM((NC, HALF, ZW), F32),
        pltpu.VMEM((32, D), F32),
        pltpu.VMEM((4, NC, ZROWS, ZW), BF16),
        pltpu.VMEM((4, NC, ZROWS, ZW), BF16),
        pltpu.VMEM((3, NC, ZROWS, ZW), BF16),
        pltpu.VMEM((3, NC, ZROWS, ZW), BF16),
        pltpu.VMEM((16, ROWS, 2 * THIRD), BF16),
        pltpu.VMEM((16, ROWS, 2 * THIRD), BF16),
        pltpu.VMEM((CLIPS, ROWS, 2 * THIRD), BF16),
        pltpu.VMEM((CLIPS, ROWS, 2 * THIRD), BF16),
        pltpu.VMEM((4, NZ, 16, SL), BF16),
        pltpu.VMEM((16, D), BF16),
        pltpu.VMEM((16, D), BF16),
        pltpu.VMEM((NZ, 16, SL), BF16),
        pltpu.VMEM((NZ, 16, SL), BF16),
        pltpu.VMEM((NZ, ROWS, SW), BF16),
        pltpu.VMEM((NZ, ROWS, SW), BF16),
        pltpu.VMEM((4, ROWS, SW), BF16),
        pltpu.VMEM((4, ROWS, SW), BF16),
        pltpu.VMEM((3, ROWS, SW), BF16),
        pltpu.VMEM((3, ROWS, SW), BF16),
        pltpu.VMEM((CH, D), F32),
        pltpu.VMEM((CH, D), BF16),
        pltpu.VMEM((32, D), BF16),
        pltpu.VMEM((HALF, NC * ZW), F32),
        pltpu.VMEM((8, 128), F32),
        pltpu.VMEM((CLIPS, 8, 128), F32),
        pltpu.VMEM((CH, TOK), BF16),
        pltpu.VMEM((TOK, CH), BF16),
        pltpu.VMEM((TOK, D), BF16),
        pltpu.VMEM((1, D), F32),
        pltpu.VMEM((8, 128), F32),
        pltpu.VMEM((TOK, H), F32),
        pltpu.VMEM((TOK, D), BF16),
        pltpu.VMEM((TOK, H), BF16),
        pltpu.VMEM((ROWS, SL), F32),
        pltpu.VMEM((CH, D), F32),
        dma((16,)), dma((7,)), dma((8,)), dma((NC,)), dma((NC,)), dma, dma,
        dma((9,)), dma((5,)), dma((16,)), dma((16,)), dma((16,)),
        dma((NZ,)), dma((NZ,)), dma((4,)), dma((4,)), dma((3,)), dma((3,)),
        dma((4 * NC,)), dma((4 * NC,)), dma((3 * NC,)), dma((3 * NC,)),
        dma((16,)), dma((16,)), dma((8,)), dma((8,)), dma((8,)), dma, dma, dma, dma, dma((7,)), dma((8,)), dma((7,)), dma((8,)), dma((3,)), dma((4,)),
    ]
    return pl.pallas_call(
        kernel,
        name="fused_step",
        out_shape=(
            jax.ShapeDtypeStruct((TOK, D), BF16),
            jax.ShapeDtypeStruct((TOK, H), BF16),
            jax.ShapeDtypeStruct((ROWS, SL), F32),
            jax.ShapeDtypeStruct((CH, D), F32),
        ),
        in_specs=[anyspace] * 11,
        out_specs=(anyspace, anyspace, anyspace, anyspace),
        scratch_shapes=scratch,
        compiler_params=pltpu.CompilerParams(
            collective_id=0, has_side_effects=True, vmem_limit_bytes=58 * 2**20
        ),
    )(step, rewards, lat, noi, vc, vu, ew, gate, vals, w, cot)


def copy_kernel(bo, ga, gw, ge, bo_o, ga_o, gw_o, ge_o, v0, v1, v2, v3, ins, outs):
    loads, stores = [], []
    n = 0
    for src, mid, dst, parts in ((bo, v0, bo_o, 4), (ga, v1, ga_o, 2), (ge, v3, ge_o, 2), (gw, v2, gw_o, 1)):
        rows = src.shape[0] // parts
        for p in range(parts):
            at = pl.ds(p * rows, rows)
            loads.append(pltpu.make_async_copy(src.at[at], mid.at[at], ins.at[n]))
            stores.append(pltpu.make_async_copy(mid.at[at], dst.at[at], outs.at[n]))
            n += 1
    for c in loads:
        c.start()
    for a, b in zip(loads, stores):
        a.wait()
        b.start()
    for c in stores:
        c.wait()


def copied(*arrays):
    anyspace = pl.BlockSpec(memory_space=pl.ANY)
    return pl.pallas_call(
        copy_kernel,
        name="results",
        out_shape=tuple(jax.ShapeDtypeStruct(a.shape, a.dtype) for a in arrays),
        in_specs=[anyspace] * 4,
        out_specs=(anyspace,) * 4,
        scratch_shapes=[pltpu.VMEM(a.shape, a.dtype) for a in arrays]
        + [pltpu.SemaphoreType.DMA((9,)), pltpu.SemaphoreType.DMA((9,))],
        compiler_params=pltpu.CompilerParams(vmem_limit_bytes=60 * 2**20),
    )(*arrays)


def local(latent, sample_noise, vel_cond, vel_uncond, step_index, embed_w, gate_scale, attn_vals, out_w, cotangent, rewards):
    bo, ga, gw, ge = copied(*fused(
        step_index, rewards, latent[0], sample_noise[0], vel_cond[0], vel_uncond[0], embed_w,
        gate_scale, attn_vals[0], out_w, cotangent[0],
    ))
    return bo[None], ga[None], gw, ge[None]


def solution(mesh):
    in_specs = (
        P("clip", None, "seq"),
        P("clip", None, "seq"),
        P("clip", None, "seq"),
        P("clip", None, "seq"),
        P(),
        P(),
        P("clip", None),
        P("clip", "seq", None),
        P(None, "clip"),
        P("clip", "seq", None),
        P("clip"),
    )
    out_specs = (
        P("clip", "seq", None),
        P("clip", "seq", None),
        P("seq", "clip"),
        P("clip", None, None),
    )
    return jax.shard_map(local, mesh=mesh, in_specs=in_specs, out_specs=out_specs, check_vma=False)
```

```python
import jax
import jax.numpy as jnp
from jax import lax
from jax.experimental import pallas as pl
from jax.experimental.pallas import tpu as pltpu
from jax.sharding import PartitionSpec as P

NSTEPS = 16
SHIFT_FACTOR = 7.0
GUIDANCE = 6.0
NOISE_LEVEL = 0.3

D = 3072
H = 1536
CH = 64
TOK = 256
NX, NZ = 4, 8
CLIPS = 8
SL = D // CLIPS
HALF = H // 2
ROWS = 48
ZROWS = 2 * ROWS
NC = 4
CC = D // NC
TILE = 256
QR = H // 4
THIRD = SL // 3
ZW = 3 * THIRD
SW = NC * ZW

MESH = pl.DeviceIdType.MESH


def mwidth(j):
    return 2 * THIRD if j % 2 else THIRD


def swidth(j):
    return SL - mwidth(j)


def soffset(j):
    return (j // 4) * 2 * ZW + (0, 2 * THIRD, 4 * THIRD, 3 * THIRD)[j % 4]

F32, BF16 = jnp.float32, jnp.bfloat16


def sigma_level(index):
    tval = 1.0 - index.astype(F32) / NSTEPS
    return SHIFT_FACTOR * tval / (1.0 + (SHIFT_FACTOR - 1.0) * tval)


def dev(x, h, lo, z, core):
    return (h * NX + x, z * 4 + lo * 2 + core)


def kernel(
    step_in, rew_in, lat_in, noi_in, vc_in, vu_in, ew_in, gate_in, vals_ref, w_ref, cot_ref,
    bo_out, ga_out, gw_out, ge_out,
    step_ref, rew_ref, lat_ref, noi_ref, vc_ref, vu_ref, ew_ref, gate_ref, vals_v, cot2, a2, vts, wf, gs, es, zls, zlr, zss, zsr, fs, fr, fss, frs, ef, ehs, ehr, e2s, e2r,
    sss, ssr, szls, szlr, szss, szsr,
    e_own, eo, er, gside, rsb, rrb, samp, samp_t, branch, gadv, advb, ga_acc, bo_ref, ga_ref, gw_ref, ge_ref,
    loc, r_s, r_r, cot_s, cot_r, a2_s, a2_r, wx_s, wy_s, wc_s, w_r, wc_r,
    ss_s, ss_r, szl_s, szl_r, szs_s, szs_r, zl_s, zl_r, zs_s, zs_r, f_s, f_r, f2_s, f2_r, bo_s, e1_s, e1_r, eh_s, eh_r, e2_s, e2_r, e3_s, e3_r, e4_s, e4_r,
):
    clip = lax.axis_index("clip")
    seq = lax.axis_index("seq")
    h, x = lax.div(clip, NX), lax.rem(clip, NX)
    z, lo, core = lax.div(seq, 4), lax.rem(lax.div(seq, 2), 2), lax.rem(seq, 2)
    oc, olo, oh = 1 - core, 1 - lo, 1 - h
    sgn = 1 - 2 * core

    def xr(n):
        return lax.rem(x + n + NX, NX)

    def zr(n):
        return lax.rem(z + n + NZ, NZ)

    def rcopy(src, dst, ss, rs, to):
        return pltpu.make_async_remote_copy(
            src_ref=src, dst_ref=dst, send_sem=ss, recv_sem=rs, device_id=to, device_id_type=MESH
        )

    bar = pltpu.get_barrier_semaphore()
    me16 = clip * 2 + lo
    partners = []
    for r in range(1, 16):
        o = lax.rem(me16 + r, 16)
        oclip, olo_ = lax.div(o, 2), lax.rem(o, 2)
        partners.append((oclip, z * 4 + olo_ * 2 + core))
    for r in range(1, NZ):
        partners.append(dev(x, h, lo, zr(r), core))
    partners.append(dev(x, h, lo, z, oc))
    partners.append(dev(x, h, olo, z, oc))
    for p in partners:
        pl.semaphore_signal(bar, inc=1, device_id=p, device_id_type=MESH)

    ld_vals = pltpu.make_async_copy(vals_ref, vals_v, loc.at[0])
    ld_cot = pltpu.make_async_copy(cot_ref, cot2.at[pl.ds(0, TOK)], loc.at[1])
    ld_w = pltpu.make_async_copy(w_ref, wf.at[clip], loc.at[2])
    ld_vals.start()
    ld_cot.start()
    ld_w.start()
    small = ((step_in, step_ref), (rew_in, rew_ref), (lat_in, lat_ref), (noi_in, noi_ref),
             (vc_in, vc_ref), (vu_in, vu_ref), (ew_in, ew_ref), (gate_in, gate_ref))
    ld_small = [pltpu.make_async_copy(a, b, loc.at[8 + i]) for i, (a, b) in enumerate(small)]
    for cp in ld_small:
        cp.start()

    for cp in ld_small[:6]:
        cp.wait()
    rsb[...] = jnp.full((8, 128), rew_ref[0], F32)
    rrb[clip] = jnp.full((8, 128), rew_ref[0], F32)
    idx = jnp.full((1, TOK), step_ref[0], jnp.int32)
    sig_now = sigma_level(idx)
    sig_next = sigma_level(idx + 1)
    uncond = vu_ref[...].astype(F32)
    guided = uncond + GUIDANCE * (vc_ref[...].astype(F32) - uncond)
    spread = NOISE_LEVEL * jnp.sqrt(sig_now - sig_next)
    sampled = lat_ref[...] + (sig_next - sig_now) * guided + spread * noi_ref[...]
    samp_t[...] = sampled.T.astype(BF16)
    samp_b = sampled.astype(BF16)
    samp[...] = samp_b

    ld_vals.wait()
    for b in range(H // 384):
        vt = vals_v[:, b * 384:(b + 1) * 384].T
        for q in range(8):
            s = b * 8 + q
            zz, ll, cc = s // 4, (s // 2) % 2, s % 2
            vts[cc, pl.ds(zz * ZROWS + ll * ROWS, ROWS), :] = vt[q * ROWS:(q + 1) * ROWS]
    a2[:, pl.ds(0, TOK)] = vts[core]

    pl.semaphore_wait(bar, len(partners))

    core_dev = dev(x, h, lo, z, oc)
    cp_a2 = rcopy(vts.at[oc], a2.at[:, pl.ds(TOK, TOK)], a2_s, a2_r, core_dev)
    cp_a2.start()
    cp_cot = []
    for k in range(NC):
        cols = pl.ds(k * CC, CC)
        cp = rcopy(cot_ref.at[:, cols], cot2.at[pl.ds(TOK, TOK), cols], cot_s.at[k], cot_r.at[k], core_dev)
        cp.start()
        cp_cot.append(cp)
    rsends = []
    for r in range(1, CLIPS):
        c = lax.rem(clip + r, CLIPS)
        cp = rcopy(rsb, rrb.at[clip], r_s.at[r - 1], r_r.at[clip], (c, seq))
        cp.start()
        rsends.append(cp)

    side = dev(x, h, olo, z, core)
    cross = dev(x, oh, olo, z, core)

    def quarter(i):
        return pl.ds(pl.multiple_of((core * 2 + i) * QR, QR), QR)

    def w_own(i, ss, to):
        return rcopy(w_ref.at[quarter(i)], wf.at[clip, quarter(i)], ss, w_r.at[clip * 2 + i], to)

    def w_fwd(slot, i, ss, to):
        return rcopy(wf.at[slot, quarter(i)], wf.at[slot, quarter(i)], ss, w_r.at[slot * 2 + i], to)

    xp = dev(xr(1), h, lo, z, core)
    xm = dev(xr(-1), h, lo, z, core)
    xs = dev(xr(sgn), h, lo, z, core)
    for i in range(2):
        w_own(i, wx_s.at[2 * i], xp).start()
        w_own(i, wx_s.at[2 * i + 1], xm).start()
        w_own(i, wy_s.at[i], cross).start()

    def a_slot(i):
        return h * NX + xr(i)

    def b_slot(i):
        return oh * NX + xr(i)

    def w_core(slot, i):
        n = slot * 2 + i
        return rcopy(wf.at[slot, quarter(i)], wf.at[slot, quarter(i)], wc_s.at[n], wc_r.at[n], core_dev)

    def w_core_other(slot, i):
        n = slot * 2 + i
        rows = pl.ds(pl.multiple_of((oc * 2 + i) * QR, QR), QR)
        return rcopy(wf.at[slot, rows], wf.at[slot, rows], wc_s.at[n], wc_r.at[n], core_dev)

    def got(slot, i):
        w_fwd(slot, i, wx_s.at[0], xp).wait_recv()
        w_core(slot, i).start()

    ld_cot.wait()

    zl_dev = dev(x, h, lo, zr(sgn), core)
    zs_dev = dev(x, h, lo, zr(-sgn), core)

    def zlong(t, k):
        n = t * NC + k
        return rcopy(zls.at[t, k], zlr.at[t, k], zl_s.at[n], zl_r.at[n], zl_dev)

    def zshort(t, k):
        n = t * NC + k
        return rcopy(zss.at[t, k], zsr.at[t, k], zs_s.at[n], zs_r.at[n], zs_dev)

    def zrows(d):
        return pl.ds(pl.multiple_of(d * ZROWS, ZROWS), ZROWS)

    def zadd(t, k, d, out, got_ref):
        v = gs[k, zrows(d), :]
        if t:
            v = v + got_ref[t - 1, k].astype(F32)
        out[t, k] = v.astype(BF16)

    def zstep(t, k):
        if t:
            zlong(t - 1, k).wait_recv()
        zadd(t, k, zr(sgn * (4 - t)), zls, zlr)
        zlong(t, k).start()
        if t < 3:
            if t:
                zshort(t - 1, k).wait_recv()
            zadd(t, k, zr(-sgn * (3 - t)), zss, zsr)
            zshort(t, k).start()

    def lrows(d, l):
        return pl.ds(pl.multiple_of(d * ZROWS + l * ROWS, ROWS), ROWS)

    def sown(d, l):
        return gside[lrows(d, l), :]

    sorder = (sgn * 4, -sgn * 3, sgn * 3, -sgn * 2, sgn * 2, -sgn, sgn, 0)

    me4 = core * 2 + lo

    def e3_copy(r):
        return rcopy(ef.at[me4, z], ef.at[me4, z], e3_s.at[r - 1], e3_r.at[z], dev(x, h, lo, zr(r), core))

    def e4_copy(i):
        to = [side, core_dev, dev(x, h, olo, z, oc)][i]
        return rcopy(ef.at[me4], ef.at[me4], e4_s.at[i], e4_r.at[me4], to)

    def fs_copy(j):
        w = pl.ds(0, swidth(j))
        return rcopy(fss.at[j, :, w], frs.at[clip, :, w], f2_s.at[j], f2_r.at[clip], (j, seq))

    def side_copy(i):
        return rcopy(sss.at[i], ssr.at[i], ss_s.at[i], ss_r.at[i], side)

    def side_send(first, end):
        for i in range(first, end):
            sss[i] = sown(zr(sorder[i]), olo).astype(BF16)
            side_copy(i).start()

    def slong(t):
        return rcopy(szls.at[t], szlr.at[t], szl_s.at[t], szl_r.at[t], zl_dev)

    def sshort(t):
        return rcopy(szss.at[t], szsr.at[t], szs_s.at[t], szs_r.at[t], zs_dev)

    def splong(t):
        side_copy(2 * t).wait_recv()
        v = sown(zr(sgn * (4 - t)), lo) + ssr[2 * t].astype(F32)
        if t:
            slong(t - 1).wait_recv()
            v = v + szlr[t - 1].astype(F32)
        szls[t] = v.astype(BF16)
        slong(t).start()

    def spshort(t):
        side_copy(2 * t + 1).wait_recv()
        v = sown(zr(-sgn * (3 - t)), lo) + ssr[2 * t + 1].astype(F32)
        if t:
            sshort(t - 1).wait_recv()
            v = v + szsr[t - 1].astype(F32)
        szss[t] = v.astype(BF16)
        sshort(t).start()

    def sfinal():
        side_copy(7).wait_recv()
        slong(3).wait_recv()
        sshort(2).wait_recv()
        v = sown(z, lo) + ssr[7].astype(F32) + szlr[3].astype(F32) + szsr[2].astype(F32)
        for j in range(CLIPS):
            o, w, c = j * SL + mwidth(j), swidth(j), soffset(j)
            fss[j, :, :w] = (v[:, c:c + w] * gadv[:, o:o + w]).astype(BF16)

            @pl.when(clip != j)
            def _():
                fs_copy(j).start()

    def eh_copy():
        return rcopy(ehs, ehr, eh_s, eh_r, side)

    def e2_copy(r):
        return rcopy(e2s.at[zr(r)], e2r.at[z], e2_s.at[r - 1], e2_r.at[z], dev(x, h, lo, zr(r), core))

    def e_two():
        eh_copy().wait_recv()
        part = es[pl.ds(pl.multiple_of(lo * 16, 16), 16), :] + ehr[...].astype(F32)
        for d in range(NZ):
            e2s[d] = part[:, d * SL:(d + 1) * SL].astype(BF16)
        for r in range(1, NZ):
            e2_copy(r).start()
        e2r[z] = e2s[z]

    def e_three():
        for r in range(1, NZ):
            o = zr(r)
            rcopy(e2s.at[o], e2r.at[o], e2_s.at[r - 1], e2_r.at[o], dev(x, h, lo, o, core)).wait_recv()
        tot = e2r[0].astype(F32)
        for d in range(1, NZ):
            tot = tot + e2r[d].astype(F32)
        ef[me4, z] = tot.astype(BF16)
        for r in range(1, NZ):
            e3_copy(r).start()

    def advantage():
        for r in range(1, CLIPS):
            c = lax.rem(clip + r, CLIPS)
            rcopy(rsb, rrb.at[c], r_s.at[r - 1], r_r.at[c], (c, seq)).wait_recv()
        total = rrb[0]
        for c in range(1, CLIPS):
            total = total + rrb[c]
        adv = rrb[clip] - total / CLIPS
        advb[...] = adv
        adv1 = adv[0:1, 0:1]
        ld_small[7].wait()
        gadv[...] = gate_ref[...] * adv1

    def e_first():
        def tile(j, carry):
            cols = pl.ds(pl.multiple_of(j * TILE, TILE), TILE)
            g = jnp.dot(samp[...], cot2[pl.ds(0, TOK), cols], preferred_element_type=F32)
            e_own[:, cols] = g
            eo[:, cols] = g.astype(BF16)
            return carry
        lax.fori_loop(0, D // TILE, tile, 0)
        e1_copy().start()

    def e1_copy():
        rows = pl.ds(pl.multiple_of(oc * 32, 32), 32)
        return rcopy(eo.at[rows], er, e1_s, e1_r, core_dev)

    def e_sum():
        e1_copy().wait_recv()
        es[...] = e_own[pl.ds(pl.multiple_of(core * 32, 32), 32), :] + er[...].astype(F32)
        ehs[...] = es[pl.ds(pl.multiple_of(olo * 16, 16), 16), :].astype(BF16)
        eh_copy().start()

    def dot_cols(*pieces):
        parts = [cot2[:, a:a + w] for a, w in pieces]
        rhs = parts[0] if len(parts) == 1 else jnp.concatenate(parts, axis=1)
        return jnp.dot(a2[...], rhs, preferred_element_type=F32)

    def g_chunk(k):
        gs[k, :, :2 * THIRD] = dot_cols(((2 * k + 1) * SL, 2 * THIRD))
        gs[k, :, 2 * THIRD:] = dot_cols((2 * k * SL, THIRD))

    def g_side():
        for m in range(2):
            o = m * 2 * ZW
            j = 4 * m
            gside[:, o:o + 2 * THIRD] = dot_cols((j * SL + THIRD, 2 * THIRD))
            gside[:, o + 2 * THIRD:o + 4 * THIRD] = dot_cols(
                ((j + 1) * SL + 2 * THIRD, THIRD), ((j + 3) * SL + 2 * THIRD, THIRD)
            )
            gside[:, o + 4 * THIRD:o + 6 * THIRD] = dot_cols(((j + 2) * SL + THIRD, 2 * THIRD))

    def f_copy(q):
        to = (q // 2, z * 4 + (q % 2) * 2 + core)
        w = pl.ds(0, mwidth(q // 2))
        return rcopy(fs.at[q, :, w], fr.at[me16, :, w], f_s.at[q], f_r.at[me16], to)

    def final(k):
        zlong(3, k).wait_recv()
        zshort(2, k).wait_recv()
        both = gs[k, zrows(z), :] + zlr[3, k].astype(F32) + zsr[2, k].astype(F32)
        for j in range(2):
            jj = 2 * k + j
            w = mwidth(jj)
            r = both[:, :w] if j else both[:, 2 * THIRD:]
            r = r * gadv[:, jj * SL:jj * SL + w]
            for l in range(2):
                q = (2 * k + j) * 2 + l
                fs[q, :, :w] = r[l * ROWS:(l + 1) * ROWS].astype(BF16)

                @pl.when(me16 != q)
                def _():
                    f_copy(q).start()

    def bo_copy(slot):
        cols = pl.ds(pl.multiple_of(slot * SL, SL), SL)
        return pltpu.make_async_copy(bo_ref.at[:, cols], bo_out.at[:, cols], bo_s.at[slot])

    def w_use(slot, first=False, own=False, last=False):
        if own:
            ld_w.wait()
        else:
            w_core_other(slot, 0).wait_recv()
            w_core_other(slot, 1).wait_recv()
        cols = pl.ds(pl.multiple_of(slot * SL, SL), SL)
        proj = jnp.dot(vals_v[...], wf[slot], preferred_element_type=F32)
        emb = jnp.dot(samp_t[...], ew_ref[:, cols], preferred_element_type=F32)
        bo_ref[:, cols] = (emb + gate_ref[:, cols] * proj).astype(BF16)
        br = branch[:, cols]
        bo_copy(slot).start()
        for i in range(2):
            half = slice(i * HALF, (i + 1) * HALF)
            g = lax.dot_general(br, wf[slot, half], (((1,), (1,)), ((), ())), preferred_element_type=F32)
            if first:
                ga_acc[:, half] = g
            elif last:
                ga_ref[:, half] = (ga_acc[:, half] + g).astype(BF16)
            else:
                ga_acc[:, half] += g

    def e_four():
        for r in range(1, NZ):
            o = zr(r)
            rcopy(ef.at[me4, o], ef.at[me4, o], e3_s.at[r - 1], e3_r.at[o], dev(x, h, lo, o, core)).wait_recv()
        for i in range(3):
            e4_copy(i).start()

    def e_five():
        for i, q in enumerate((core * 2 + olo, oc * 2 + lo, oc * 2 + olo)):
            rcopy(ef.at[q], ef.at[q], e4_s.at[i], e4_r.at[q], side).wait_recv()
        for q in range(4):
            for d in range(NZ):
                ge_ref[q * 16:(q + 1) * 16, d * SL:(d + 1) * SL] = ef[q, d].astype(F32) * advb[0:1, 0:1]
        pltpu.make_async_copy(ge_ref, ge_out, loc.at[4]).start()

    def stage_1():
        got(a_slot(1), 0)
        got(a_slot(3), 0)
        w_fwd(h * NX + xr(-sgn), 0, wx_s.at[4], xs).start()
        w_fwd(a_slot(1), 0, wy_s.at[2], cross).start()
        w_fwd(a_slot(3), 0, wy_s.at[3], cross).start()

    def stage_2():
        got(a_slot(1), 1)
        got(a_slot(3), 1)
        w_fwd(h * NX + xr(-sgn), 1, wx_s.at[5], xs).start()

    def stage_2b():
        got(b_slot(0), 0)
        got(b_slot(0), 1)
        w_fwd(b_slot(0), 1, wx_s.at[6], xp).start()
        w_fwd(b_slot(0), 1, wx_s.at[7], xm).start()

    def stage_3():
        got(a_slot(2), 0)
        w_fwd(a_slot(2), 0, wy_s.at[4], cross).start()

    def stage_4():
        got(a_slot(2), 1)

    def stage_5(i):
        got(b_slot(i), 0)

    def stage_6():
        got(b_slot(1), 1)
        got(b_slot(3), 1)
        w_fwd(oh * NX + xr(-sgn), 1, wx_s.at[8], xs).start()

    def stage_8():
        got(b_slot(2), 1)

    e_first()
    cp_a2.wait_recv()
    cp_cot[0].wait_recv()
    g_chunk(0)
    zstep(0, 0)
    cp_cot[2].wait_recv()
    g_chunk(2)
    zstep(0, 2)
    cp_cot[1].wait_recv()
    cp_cot[3].wait_recv()
    g_side()
    side_send(0, 2)
    e_sum()
    side_send(2, 8)
    g_chunk(1)
    zstep(0, 1)
    g_chunk(3)
    zstep(0, 3)
    stage_1()
    zstep(1, 2)
    advantage()
    zstep(1, 0)
    ld_small[6].wait()
    scaled = (cot2[pl.ds(0, TOK), :].astype(F32) * advb[0:1, 0:1]).astype(BF16)
    branch[...] = (scaled.astype(F32) * gate_ref[...]).astype(BF16)
    splong(0)
    zstep(1, 3)
    zstep(1, 1)
    stage_2b()
    e_two()
    zstep(2, 2)
    spshort(0)
    stage_2()
    zstep(2, 0)
    w_use(b_slot(0), first=True)
    splong(1)
    zstep(2, 3)
    stage_3()
    w_use(clip, own=True)
    zstep(2, 1)
    w_use(a_slot(1))
    stage_6()
    e_three()
    stage_5(1)
    spshort(1)
    zstep(3, 2)
    stage_5(3)
    w_use(a_slot(3))
    splong(2)
    stage_4()
    zstep(3, 0)
    zstep(3, 3)
    w_use(b_slot(1))
    zstep(3, 1)
    stage_8()
    spshort(2)
    stage_5(2)
    splong(3)
    e_four()
    final(2)
    final(3)
    final(0)
    final(1)
    w_use(b_slot(3))
    sfinal()
    w_use(b_slot(2))
    w_use(a_slot(2), last=True)
    pltpu.make_async_copy(ga_ref, ga_out, loc.at[7]).start()
    e_five()

    for cp in rsends:
        cp.wait_send()
    for cp in cp_cot:
        cp.wait_send()
    cp_a2.wait_send()
    for n in range(9):
        w_fwd(a_slot(1), 0, wx_s.at[n], xp).wait_send()
    for n in range(5):
        w_fwd(a_slot(1), 0, wy_s.at[n], side).wait_send()
    for i in range(2):
        for n in range(1, 4):
            w_core(a_slot(n), i).wait_send()
        for n in range(4):
            w_core(b_slot(n), i).wait_send()
    for i in range(NZ):
        side_copy(i).wait_send()
    for t in range(4):
        slong(t).wait_send()
        if t < 3:
            sshort(t).wait_send()
        for k in range(NC):
            zlong(t, k).wait_send()
            if t < 3:
                zshort(t, k).wait_send()
    for q in range(16):
        @pl.when(me16 != q)
        def _():
            f_copy(q).wait_send()
    for j in range(CLIPS):
        @pl.when(clip != j)
        def _():
            fs_copy(j).wait_send()
    e1_copy().wait_send()
    eh_copy().wait_send()
    for r in range(1, NZ):
        e2_copy(r).wait_send()
        e3_copy(r).wait_send()
    for i in range(3):
        e4_copy(i).wait_send()

    fr[me16] = fs[me16]
    frs[clip] = fss[clip]
    for par in range(2):
        @pl.when(lax.rem(clip, 2) == par)
        def _():
            wm, ws = pl.ds(0, mwidth(par)), pl.ds(0, swidth(par))
            for q in range(16):
                @pl.when(me16 != q)
                def _():
                    rcopy(fs.at[q, :, wm], fr.at[q, :, wm], f_s.at[q], f_r.at[q], core_dev).wait_recv()
            for j in range(CLIPS):
                @pl.when(clip != j)
                def _():
                    rcopy(fss.at[j, :, ws], frs.at[j, :, ws], f2_s.at[j], f2_r.at[j], core_dev).wait_recv()
            acc = fr[0, :, wm].astype(F32)
            for q in range(1, 16):
                acc = acc + fr[q, :, wm].astype(F32)
            gw_ref[:, :mwidth(par)] = acc
            acc = frs[0, :, ws].astype(F32)
            for j in range(1, CLIPS):
                acc = acc + frs[j, :, ws].astype(F32)
            gw_ref[:, mwidth(par):] = acc
    pltpu.make_async_copy(gw_ref, gw_out, loc.at[5]).start()

    pltpu.make_async_copy(ge_ref, ge_out, loc.at[4]).wait()
    pltpu.make_async_copy(gw_ref, gw_out, loc.at[5]).wait()
    for j in range(CLIPS):
        bo_copy(j).wait()
    pltpu.make_async_copy(ga_ref, ga_out, loc.at[7]).wait()


def fused(step, rewards, lat, noi, vc, vu, ew, gate, vals, w, cot):
    anyspace = pl.BlockSpec(memory_space=pl.ANY)
    dma = pltpu.SemaphoreType.DMA
    scratch = [
        pltpu.SMEM((1,), jnp.int32),
        pltpu.SMEM((1,), F32),
        pltpu.VMEM((CH, TOK), F32),
        pltpu.VMEM((CH, TOK), F32),
        pltpu.VMEM((CH, TOK), BF16),
        pltpu.VMEM((CH, TOK), BF16),
        pltpu.VMEM((CH, D), BF16),
        pltpu.VMEM((1, D), F32),
        pltpu.VMEM((TOK, H), BF16),
        pltpu.VMEM((2 * TOK, D), BF16),
        pltpu.VMEM((HALF, 2 * TOK), BF16),
        pltpu.VMEM((2, HALF, TOK), BF16),
        pltpu.VMEM((CLIPS, H, SL), BF16),
        pltpu.VMEM((NC, HALF, ZW), F32),
        pltpu.VMEM((32, D), F32),
        pltpu.VMEM((4, NC, ZROWS, ZW), BF16),
        pltpu.VMEM((4, NC, ZROWS, ZW), BF16),
        pltpu.VMEM((3, NC, ZROWS, ZW), BF16),
        pltpu.VMEM((3, NC, ZROWS, ZW), BF16),
        pltpu.VMEM((16, ROWS, 2 * THIRD), BF16),
        pltpu.VMEM((16, ROWS, 2 * THIRD), BF16),
        pltpu.VMEM((CLIPS, ROWS, 2 * THIRD), BF16),
        pltpu.VMEM((CLIPS, ROWS, 2 * THIRD), BF16),
        pltpu.VMEM((4, NZ, 16, SL), BF16),
        pltpu.VMEM((16, D), BF16),
        pltpu.VMEM((16, D), BF16),
        pltpu.VMEM((NZ, 16, SL), BF16),
        pltpu.VMEM((NZ, 16, SL), BF16),
        pltpu.VMEM((NZ, ROWS, SW), BF16),
        pltpu.VMEM((NZ, ROWS, SW), BF16),
        pltpu.VMEM((4, ROWS, SW), BF16),
        pltpu.VMEM((4, ROWS, SW), BF16),
        pltpu.VMEM((3, ROWS, SW), BF16),
        pltpu.VMEM((3, ROWS, SW), BF16),
        pltpu.VMEM((CH, D), F32),
        pltpu.VMEM((CH, D), BF16),
        pltpu.VMEM((32, D), BF16),
        pltpu.VMEM((HALF, NC * ZW), F32),
        pltpu.VMEM((8, 128), F32),
        pltpu.VMEM((CLIPS, 8, 128), F32),
        pltpu.VMEM((CH, TOK), BF16),
        pltpu.VMEM((TOK, CH), BF16),
        pltpu.VMEM((TOK, D), BF16),
        pltpu.VMEM((1, D), F32),
        pltpu.VMEM((8, 128), F32),
        pltpu.VMEM((TOK, H), F32),
        pltpu.VMEM((TOK, D), BF16),
        pltpu.VMEM((TOK, H), BF16),
        pltpu.VMEM((ROWS, SL), F32),
        pltpu.VMEM((CH, D), F32),
        dma((16,)), dma((7,)), dma((8,)), dma((NC,)), dma((NC,)), dma, dma,
        dma((9,)), dma((5,)), dma((16,)), dma((16,)), dma((16,)),
        dma((NZ,)), dma((NZ,)), dma((4,)), dma((4,)), dma((3,)), dma((3,)),
        dma((4 * NC,)), dma((4 * NC,)), dma((3 * NC,)), dma((3 * NC,)),
        dma((16,)), dma((16,)), dma((8,)), dma((8,)), dma((8,)), dma, dma, dma, dma, dma((7,)), dma((8,)), dma((7,)), dma((8,)), dma((3,)), dma((4,)),
    ]
    return pl.pallas_call(
        kernel,
        name="fused_step",
        out_shape=(
            jax.ShapeDtypeStruct((TOK, D), BF16),
            jax.ShapeDtypeStruct((TOK, H), BF16),
            jax.ShapeDtypeStruct((ROWS, SL), F32),
            jax.ShapeDtypeStruct((CH, D), F32),
        ),
        in_specs=[anyspace] * 11,
        out_specs=(anyspace, anyspace, anyspace, anyspace),
        scratch_shapes=scratch,
        compiler_params=pltpu.CompilerParams(
            collective_id=0, has_side_effects=True, vmem_limit_bytes=58 * 2**20
        ),
    )(step, rewards, lat, noi, vc, vu, ew, gate, vals, w, cot)


def copy_kernel(bo, ga, gw, ge, bo_o, ga_o, gw_o, ge_o, v0, v1, v2, v3, ins, outs):
    loads, stores = [], []
    n = 0
    for src, mid, dst, parts in ((bo, v0, bo_o, 4), (ga, v1, ga_o, 2), (ge, v3, ge_o, 2), (gw, v2, gw_o, 1)):
        rows = src.shape[0] // parts
        for p in range(parts):
            at = pl.ds(p * rows, rows)
            loads.append(pltpu.make_async_copy(src.at[at], mid.at[at], ins.at[n]))
            stores.append(pltpu.make_async_copy(mid.at[at], dst.at[at], outs.at[n]))
            n += 1
    for c in loads:
        c.start()
    for a, b in zip(loads, stores):
        a.wait()
        b.start()
    for c in stores:
        c.wait()


def copied(*arrays):
    anyspace = pl.BlockSpec(memory_space=pl.ANY)
    return pl.pallas_call(
        copy_kernel,
        name="results",
        out_shape=tuple(jax.ShapeDtypeStruct(a.shape, a.dtype) for a in arrays),
        in_specs=[anyspace] * 4,
        out_specs=(anyspace,) * 4,
        scratch_shapes=[pltpu.VMEM(a.shape, a.dtype) for a in arrays]
        + [pltpu.SemaphoreType.DMA((9,)), pltpu.SemaphoreType.DMA((9,))],
        compiler_params=pltpu.CompilerParams(vmem_limit_bytes=60 * 2**20),
    )(*arrays)


def local(latent, sample_noise, vel_cond, vel_uncond, step_index, embed_w, gate_scale, attn_vals, out_w, cotangent, rewards):
    bo, ga, gw, ge = copied(*fused(
        step_index, rewards, latent[0], sample_noise[0], vel_cond[0], vel_uncond[0], embed_w,
        gate_scale, attn_vals[0], out_w, cotangent[0],
    ))
    return bo[None], ga[None], gw, ge[None]


def solution(mesh):
    in_specs = (
        P("clip", None, "seq"),
        P("clip", None, "seq"),
        P("clip", None, "seq"),
        P("clip", None, "seq"),
        P(),
        P(),
        P("clip", None),
        P("clip", "seq", None),
        P(None, "clip"),
        P("clip", "seq", None),
        P("clip"),
    )
    out_specs = (
        P("clip", "seq", None),
        P("clip", "seq", None),
        P("seq", "clip"),
        P("clip", None, None),
    )
    return jax.shard_map(local, mesh=mesh, in_specs=in_specs, out_specs=out_specs, check_vma=False)
```

```python
import jax
import jax.numpy as jnp
from jax import lax
from jax.experimental import pallas as pl
from jax.experimental.pallas import tpu as pltpu
from jax.sharding import PartitionSpec as P

NSTEPS = 16
SHIFT_FACTOR = 7.0
GUIDANCE = 6.0
NOISE_LEVEL = 0.3

D = 3072
H = 1536
CH = 64
TOK = 256
NX, NZ = 4, 8
CLIPS = 8
SL = D // CLIPS
HALF = H // 2
ROWS = 48
ZROWS = 2 * ROWS
NC = 4
CC = D // NC
TILE = 256
QR = H // 4
THIRD = SL // 3
ZW = 3 * THIRD
SW = NC * ZW

MESH = pl.DeviceIdType.MESH


def mwidth(j):
    return 2 * THIRD if j % 2 else THIRD


def swidth(j):
    return SL - mwidth(j)


def soffset(j):
    return (j // 4) * 2 * ZW + (0, 2 * THIRD, 4 * THIRD, 3 * THIRD)[j % 4]

F32, BF16 = jnp.float32, jnp.bfloat16


def sigma_level(index):
    tval = 1.0 - index.astype(F32) / NSTEPS
    return SHIFT_FACTOR * tval / (1.0 + (SHIFT_FACTOR - 1.0) * tval)


def dev(x, h, lo, z, core):
    return (h * NX + x, z * 4 + lo * 2 + core)


def kernel(
    step_in, rew_in, lat_in, noi_in, vc_in, vu_in, ew_in, gate_in, vals_ref, w_ref, cot_ref,
    bo_out, ga_out, gw_out, ge_out,
    step_ref, rew_ref, lat_ref, noi_ref, vc_ref, vu_ref, ew_ref, gate_ref, vals_v, cot2, a2, vts, wf, gs, es, zls, zlr, zss, zsr, fs, fr, fss, frs, ef, ehs, ehr, e2s, e2r,
    sss, ssr, szls, szlr, szss, szsr,
    e_own, eo, er, gside, rsb, rrb, samp, samp_t, branch, gadv, advb, ga_acc, bo_ref, ga_ref, gw_ref, ge_ref,
    loc, r_s, r_r, cot_s, cot_r, a2_s, a2_r, wx_s, wy_s, wc_s, w_r, wc_r,
    ss_s, ss_r, szl_s, szl_r, szs_s, szs_r, zl_s, zl_r, zs_s, zs_r, f_s, f_r, f2_s, f2_r, bo_s, e1_s, e1_r, eh_s, eh_r, e2_s, e2_r, e3_s, e3_r, e4_s, e4_r,
):
    clip = lax.axis_index("clip")
    seq = lax.axis_index("seq")
    h, x = lax.div(clip, NX), lax.rem(clip, NX)
    z, lo, core = lax.div(seq, 4), lax.rem(lax.div(seq, 2), 2), lax.rem(seq, 2)
    oc, olo, oh = 1 - core, 1 - lo, 1 - h
    sgn = 1 - 2 * core

    def xr(n):
        return lax.rem(x + n + NX, NX)

    def zr(n):
        return lax.rem(z + n + NZ, NZ)

    def rcopy(src, dst, ss, rs, to):
        return pltpu.make_async_remote_copy(
            src_ref=src, dst_ref=dst, send_sem=ss, recv_sem=rs, device_id=to, device_id_type=MESH
        )

    bar = pltpu.get_barrier_semaphore()
    me16 = clip * 2 + lo
    partners = []
    for r in range(1, 16):
        o = lax.rem(me16 + r, 16)
        oclip, olo_ = lax.div(o, 2), lax.rem(o, 2)
        partners.append((oclip, z * 4 + olo_ * 2 + core))
    for r in range(1, NZ):
        partners.append(dev(x, h, lo, zr(r), core))
    partners.append(dev(x, h, lo, z, oc))
    partners.append(dev(x, h, olo, z, oc))
    for p in partners:
        pl.semaphore_signal(bar, inc=1, device_id=p, device_id_type=MESH)

    ld_vals = pltpu.make_async_copy(vals_ref, vals_v, loc.at[0])
    ld_cot = pltpu.make_async_copy(cot_ref, cot2.at[pl.ds(0, TOK)], loc.at[1])
    ld_w = pltpu.make_async_copy(w_ref, wf.at[clip], loc.at[2])
    ld_vals.start()
    ld_cot.start()
    ld_w.start()
    small = ((step_in, step_ref), (rew_in, rew_ref), (lat_in, lat_ref), (noi_in, noi_ref),
             (vc_in, vc_ref), (vu_in, vu_ref), (ew_in, ew_ref), (gate_in, gate_ref))
    ld_small = [pltpu.make_async_copy(a, b, loc.at[8 + i]) for i, (a, b) in enumerate(small)]
    for cp in ld_small:
        cp.start()

    for cp in ld_small[:6]:
        cp.wait()
    rsb[...] = jnp.full((8, 128), rew_ref[0], F32)
    rrb[clip] = jnp.full((8, 128), rew_ref[0], F32)
    idx = jnp.full((1, TOK), step_ref[0], jnp.int32)
    sig_now = sigma_level(idx)
    sig_next = sigma_level(idx + 1)
    uncond = vu_ref[...].astype(F32)
    guided = uncond + GUIDANCE * (vc_ref[...].astype(F32) - uncond)
    spread = NOISE_LEVEL * jnp.sqrt(sig_now - sig_next)
    sampled = lat_ref[...] + (sig_next - sig_now) * guided + spread * noi_ref[...]
    samp_t[...] = sampled.T.astype(BF16)
    samp_b = sampled.astype(BF16)
    samp[...] = samp_b

    ld_vals.wait()
    for b in range(H // 384):
        vt = vals_v[:, b * 384:(b + 1) * 384].T
        for q in range(8):
            s = b * 8 + q
            zz, ll, cc = s // 4, (s // 2) % 2, s % 2
            vts[cc, pl.ds(zz * ZROWS + ll * ROWS, ROWS), :] = vt[q * ROWS:(q + 1) * ROWS]
    a2[:, pl.ds(0, TOK)] = vts[core]

    pl.semaphore_wait(bar, len(partners))

    core_dev = dev(x, h, lo, z, oc)
    cp_a2 = rcopy(vts.at[oc], a2.at[:, pl.ds(TOK, TOK)], a2_s, a2_r, core_dev)
    cp_a2.start()
    cp_cot = []
    for k in range(NC):
        cols = pl.ds(k * CC, CC)
        cp = rcopy(cot_ref.at[:, cols], cot2.at[pl.ds(TOK, TOK), cols], cot_s.at[k], cot_r.at[k], core_dev)
        cp.start()
        cp_cot.append(cp)
    rsends = []
    for r in range(1, CLIPS):
        c = lax.rem(clip + r, CLIPS)
        cp = rcopy(rsb, rrb.at[clip], r_s.at[r - 1], r_r.at[clip], (c, seq))
        cp.start()
        rsends.append(cp)

    side = dev(x, h, olo, z, core)
    cross = dev(x, oh, olo, z, core)

    def quarter(i):
        return pl.ds(pl.multiple_of((core * 2 + i) * QR, QR), QR)

    def w_own(i, ss, to):
        return rcopy(w_ref.at[quarter(i)], wf.at[clip, quarter(i)], ss, w_r.at[clip * 2 + i], to)

    def w_fwd(slot, i, ss, to):
        return rcopy(wf.at[slot, quarter(i)], wf.at[slot, quarter(i)], ss, w_r.at[slot * 2 + i], to)

    xp = dev(xr(1), h, lo, z, core)
    xm = dev(xr(-1), h, lo, z, core)
    xs = dev(xr(sgn), h, lo, z, core)
    for i in range(2):
        w_own(i, wx_s.at[2 * i], xp).start()
        w_own(i, wx_s.at[2 * i + 1], xm).start()
        w_own(i, wy_s.at[i], cross).start()

    def a_slot(i):
        return h * NX + xr(i)

    def b_slot(i):
        return oh * NX + xr(i)

    def w_core(slot, i):
        n = slot * 2 + i
        return rcopy(wf.at[slot, quarter(i)], wf.at[slot, quarter(i)], wc_s.at[n], wc_r.at[n], core_dev)

    def w_core_other(slot, i):
        n = slot * 2 + i
        rows = pl.ds(pl.multiple_of((oc * 2 + i) * QR, QR), QR)
        return rcopy(wf.at[slot, rows], wf.at[slot, rows], wc_s.at[n], wc_r.at[n], core_dev)

    def got(slot, i):
        w_fwd(slot, i, wx_s.at[0], xp).wait_recv()
        w_core(slot, i).start()

    ld_cot.wait()

    zl_dev = dev(x, h, lo, zr(sgn), core)
    zs_dev = dev(x, h, lo, zr(-sgn), core)

    def zlong(t, k):
        n = t * NC + k
        return rcopy(zls.at[t, k], zlr.at[t, k], zl_s.at[n], zl_r.at[n], zl_dev)

    def zshort(t, k):
        n = t * NC + k
        return rcopy(zss.at[t, k], zsr.at[t, k], zs_s.at[n], zs_r.at[n], zs_dev)

    def zrows(d):
        return pl.ds(pl.multiple_of(d * ZROWS, ZROWS), ZROWS)

    def zadd(t, k, d, out, got_ref):
        v = gs[k, zrows(d), :]
        if t:
            v = v + got_ref[t - 1, k].astype(F32)
        out[t, k] = v.astype(BF16)

    def zstep(t, k):
        if t:
            zlong(t - 1, k).wait_recv()
        zadd(t, k, zr(sgn * (4 - t)), zls, zlr)
        zlong(t, k).start()
        if t < 3:
            if t:
                zshort(t - 1, k).wait_recv()
            zadd(t, k, zr(-sgn * (3 - t)), zss, zsr)
            zshort(t, k).start()

    def lrows(d, l):
        return pl.ds(pl.multiple_of(d * ZROWS + l * ROWS, ROWS), ROWS)

    def sown(d, l):
        return gside[lrows(d, l), :]

    sorder = (sgn * 4, -sgn * 3, sgn * 3, -sgn * 2, sgn * 2, -sgn, sgn, 0)

    me4 = core * 2 + lo

    def e3_copy(r):
        return rcopy(ef.at[me4, z], ef.at[me4, z], e3_s.at[r - 1], e3_r.at[z], dev(x, h, lo, zr(r), core))

    def e4_copy(i):
        to = [side, core_dev, dev(x, h, olo, z, oc)][i]
        return rcopy(ef.at[me4], ef.at[me4], e4_s.at[i], e4_r.at[me4], to)

    def fs_copy(j):
        w = pl.ds(0, swidth(j))
        return rcopy(fss.at[j, :, w], frs.at[clip, :, w], f2_s.at[j], f2_r.at[clip], (j, seq))

    def side_copy(i):
        return rcopy(sss.at[i], ssr.at[i], ss_s.at[i], ss_r.at[i], side)

    def side_send(first, end):
        for i in range(first, end):
            sss[i] = sown(zr(sorder[i]), olo).astype(BF16)
            side_copy(i).start()

    def slong(t):
        return rcopy(szls.at[t], szlr.at[t], szl_s.at[t], szl_r.at[t], zl_dev)

    def sshort(t):
        return rcopy(szss.at[t], szsr.at[t], szs_s.at[t], szs_r.at[t], zs_dev)

    def splong(t):
        side_copy(2 * t).wait_recv()
        v = sown(zr(sgn * (4 - t)), lo) + ssr[2 * t].astype(F32)
        if t:
            slong(t - 1).wait_recv()
            v = v + szlr[t - 1].astype(F32)
        szls[t] = v.astype(BF16)
        slong(t).start()

    def spshort(t):
        side_copy(2 * t + 1).wait_recv()
        v = sown(zr(-sgn * (3 - t)), lo) + ssr[2 * t + 1].astype(F32)
        if t:
            sshort(t - 1).wait_recv()
            v = v + szsr[t - 1].astype(F32)
        szss[t] = v.astype(BF16)
        sshort(t).start()

    def sfinal():
        side_copy(7).wait_recv()
        slong(3).wait_recv()
        sshort(2).wait_recv()
        v = sown(z, lo) + ssr[7].astype(F32) + szlr[3].astype(F32) + szsr[2].astype(F32)
        for j in range(CLIPS):
            o, w, c = j * SL + mwidth(j), swidth(j), soffset(j)
            fss[j, :, :w] = (v[:, c:c + w] * gadv[:, o:o + w]).astype(BF16)

            @pl.when(clip != j)
            def _():
                fs_copy(j).start()

    def eh_copy():
        return rcopy(ehs, ehr, eh_s, eh_r, side)

    def e2_copy(r):
        return rcopy(e2s.at[zr(r)], e2r.at[z], e2_s.at[r - 1], e2_r.at[z], dev(x, h, lo, zr(r), core))

    def e_two():
        eh_copy().wait_recv()
        part = es[pl.ds(pl.multiple_of(lo * 16, 16), 16), :] + ehr[...].astype(F32)
        for d in range(NZ):
            e2s[d] = part[:, d * SL:(d + 1) * SL].astype(BF16)
        for r in range(1, NZ):
            e2_copy(r).start()
        e2r[z] = e2s[z]

    def e_three():
        for r in range(1, NZ):
            o = zr(r)
            rcopy(e2s.at[o], e2r.at[o], e2_s.at[r - 1], e2_r.at[o], dev(x, h, lo, o, core)).wait_recv()
        tot = e2r[0].astype(F32)
        for d in range(1, NZ):
            tot = tot + e2r[d].astype(F32)
        ef[me4, z] = tot.astype(BF16)
        for r in range(1, NZ):
            e3_copy(r).start()

    def advantage():
        for r in range(1, CLIPS):
            c = lax.rem(clip + r, CLIPS)
            rcopy(rsb, rrb.at[c], r_s.at[r - 1], r_r.at[c], (c, seq)).wait_recv()
        total = rrb[0]
        for c in range(1, CLIPS):
            total = total + rrb[c]
        adv = rrb[clip] - total / CLIPS
        advb[...] = adv
        adv1 = adv[0:1, 0:1]
        ld_small[7].wait()
        gadv[...] = gate_ref[...] * adv1

    def e_first():
        def tile(j, carry):
            cols = pl.ds(pl.multiple_of(j * TILE, TILE), TILE)
            g = jnp.dot(samp[...], cot2[pl.ds(0, TOK), cols], preferred_element_type=F32)
            e_own[:, cols] = g
            eo[:, cols] = g.astype(BF16)
            return carry
        lax.fori_loop(0, D // TILE, tile, 0)
        e1_copy().start()

    def e1_copy():
        rows = pl.ds(pl.multiple_of(oc * 32, 32), 32)
        return rcopy(eo.at[rows], er, e1_s, e1_r, core_dev)

    def e_sum():
        e1_copy().wait_recv()
        es[...] = e_own[pl.ds(pl.multiple_of(core * 32, 32), 32), :] + er[...].astype(F32)
        ehs[...] = es[pl.ds(pl.multiple_of(olo * 16, 16), 16), :].astype(BF16)
        eh_copy().start()

    def dot_cols(*pieces):
        parts = [cot2[:, a:a + w] for a, w in pieces]
        rhs = parts[0] if len(parts) == 1 else jnp.concatenate(parts, axis=1)
        return jnp.dot(a2[...], rhs, preferred_element_type=F32)

    def g_chunk(k):
        gs[k, :, :2 * THIRD] = dot_cols(((2 * k + 1) * SL, 2 * THIRD))
        gs[k, :, 2 * THIRD:] = dot_cols((2 * k * SL, THIRD))

    def g_side():
        for m in range(2):
            o = m * 2 * ZW
            j = 4 * m
            gside[:, o:o + 2 * THIRD] = dot_cols((j * SL + THIRD, 2 * THIRD))
            gside[:, o + 2 * THIRD:o + 4 * THIRD] = dot_cols(
                ((j + 1) * SL + 2 * THIRD, THIRD), ((j + 3) * SL + 2 * THIRD, THIRD)
            )
            gside[:, o + 4 * THIRD:o + 6 * THIRD] = dot_cols(((j + 2) * SL + THIRD, 2 * THIRD))

    def f_copy(q):
        to = (q // 2, z * 4 + (q % 2) * 2 + core)
        w = pl.ds(0, mwidth(q // 2))
        return rcopy(fs.at[q, :, w], fr.at[me16, :, w], f_s.at[q], f_r.at[me16], to)

    def final(k):
        zlong(3, k).wait_recv()
        zshort(2, k).wait_recv()
        both = gs[k, zrows(z), :] + zlr[3, k].astype(F32) + zsr[2, k].astype(F32)
        for j in range(2):
            jj = 2 * k + j
            w = mwidth(jj)
            r = both[:, :w] if j else both[:, 2 * THIRD:]
            r = r * gadv[:, jj * SL:jj * SL + w]
            for l in range(2):
                q = (2 * k + j) * 2 + l
                fs[q, :, :w] = r[l * ROWS:(l + 1) * ROWS].astype(BF16)

                @pl.when(me16 != q)
                def _():
                    f_copy(q).start()

    def bo_copy(slot):
        cols = pl.ds(pl.multiple_of(slot * SL, SL), SL)
        return pltpu.make_async_copy(bo_ref.at[:, cols], bo_out.at[:, cols], bo_s.at[slot])

    def w_use(slot, first=False, own=False, last=False):
        if own:
            ld_w.wait()
        else:
            w_core_other(slot, 0).wait_recv()
            w_core_other(slot, 1).wait_recv()
        cols = pl.ds(pl.multiple_of(slot * SL, SL), SL)
        proj = jnp.dot(vals_v[...], wf[slot], preferred_element_type=F32)
        emb = jnp.dot(samp_t[...], ew_ref[:, cols], preferred_element_type=F32)
        bo_ref[:, cols] = (emb + gate_ref[:, cols] * proj).astype(BF16)
        br = branch[:, cols]
        bo_copy(slot).start()
        for i in range(2):
            half = slice(i * HALF, (i + 1) * HALF)
            g = lax.dot_general(br, wf[slot, half], (((1,), (1,)), ((), ())), preferred_element_type=F32)
            if first:
                ga_acc[:, half] = g
            elif last:
                ga_ref[:, half] = (ga_acc[:, half] + g).astype(BF16)
            else:
                ga_acc[:, half] += g

    def e_four():
        for r in range(1, NZ):
            o = zr(r)
            rcopy(ef.at[me4, o], ef.at[me4, o], e3_s.at[r - 1], e3_r.at[o], dev(x, h, lo, o, core)).wait_recv()
        for i in range(3):
            e4_copy(i).start()

    def e_five():
        for i, q in enumerate((core * 2 + olo, oc * 2 + lo, oc * 2 + olo)):
            rcopy(ef.at[q], ef.at[q], e4_s.at[i], e4_r.at[q], side).wait_recv()
        for q in range(4):
            for d in range(NZ):
                ge_ref[q * 16:(q + 1) * 16, d * SL:(d + 1) * SL] = ef[q, d].astype(F32) * advb[0:1, 0:1]
        pltpu.make_async_copy(ge_ref, ge_out, loc.at[4]).start()

    def stage_1():
        got(a_slot(1), 0)
        got(a_slot(3), 0)
        w_fwd(h * NX + xr(-sgn), 0, wx_s.at[4], xs).start()
        w_fwd(a_slot(1), 0, wy_s.at[2], cross).start()
        w_fwd(a_slot(3), 0, wy_s.at[3], cross).start()

    def stage_2():
        got(a_slot(1), 1)
        got(a_slot(3), 1)
        w_fwd(h * NX + xr(-sgn), 1, wx_s.at[5], xs).start()

    def stage_2b():
        got(b_slot(0), 0)
        got(b_slot(0), 1)
        w_fwd(b_slot(0), 1, wx_s.at[6], xp).start()
        w_fwd(b_slot(0), 1, wx_s.at[7], xm).start()

    def stage_3():
        got(a_slot(2), 0)
        w_fwd(a_slot(2), 0, wy_s.at[4], cross).start()

    def stage_4():
        got(a_slot(2), 1)

    def stage_5(i):
        got(b_slot(i), 0)

    def stage_6():
        got(b_slot(1), 1)
        got(b_slot(3), 1)
        w_fwd(oh * NX + xr(-sgn), 1, wx_s.at[8], xs).start()

    def stage_8():
        got(b_slot(2), 1)

    e_first()
    cp_a2.wait_recv()
    cp_cot[0].wait_recv()
    g_chunk(0)
    zstep(0, 0)
    cp_cot[2].wait_recv()
    g_chunk(2)
    zstep(0, 2)
    cp_cot[1].wait_recv()
    cp_cot[3].wait_recv()
    g_side()
    side_send(0, 2)
    e_sum()
    side_send(2, 8)
    g_chunk(1)
    zstep(0, 1)
    g_chunk(3)
    zstep(0, 3)
    stage_1()
    zstep(1, 2)
    advantage()
    zstep(1, 0)
    ld_small[6].wait()
    scaled = (cot2[pl.ds(0, TOK), :].astype(F32) * advb[0:1, 0:1]).astype(BF16)
    branch[...] = (scaled.astype(F32) * gate_ref[...]).astype(BF16)
    splong(0)
    zstep(1, 3)
    zstep(1, 1)
    stage_2b()
    e_two()
    zstep(2, 2)
    spshort(0)
    stage_2()
    zstep(2, 0)
    w_use(b_slot(0), first=True)
    splong(1)
    zstep(2, 3)
    stage_3()
    w_use(clip, own=True)
    zstep(2, 1)
    w_use(a_slot(1))
    stage_6()
    e_three()
    stage_5(1)
    spshort(1)
    zstep(3, 2)
    stage_5(3)
    w_use(a_slot(3))
    splong(2)
    stage_4()
    zstep(3, 0)
    zstep(3, 3)
    w_use(b_slot(1))
    zstep(3, 1)
    stage_8()
    spshort(2)
    stage_5(2)
    splong(3)
    e_four()
    final(2)
    final(3)
    final(0)
    final(1)
    w_use(b_slot(3))
    sfinal()
    w_use(b_slot(2))
    w_use(a_slot(2), last=True)
    pltpu.make_async_copy(ga_ref, ga_out, loc.at[7]).start()
    e_five()

    for cp in rsends:
        cp.wait_send()
    for cp in cp_cot:
        cp.wait_send()
    cp_a2.wait_send()
    for n in range(9):
        w_fwd(a_slot(1), 0, wx_s.at[n], xp).wait_send()
    for n in range(5):
        w_fwd(a_slot(1), 0, wy_s.at[n], side).wait_send()
    for i in range(2):
        for n in range(1, 4):
            w_core(a_slot(n), i).wait_send()
        for n in range(4):
            w_core(b_slot(n), i).wait_send()
    for i in range(NZ):
        side_copy(i).wait_send()
    for t in range(4):
        slong(t).wait_send()
        if t < 3:
            sshort(t).wait_send()
        for k in range(NC):
            zlong(t, k).wait_send()
            if t < 3:
                zshort(t, k).wait_send()
    for q in range(16):
        @pl.when(me16 != q)
        def _():
            f_copy(q).wait_send()
    for j in range(CLIPS):
        @pl.when(clip != j)
        def _():
            fs_copy(j).wait_send()
    e1_copy().wait_send()
    eh_copy().wait_send()
    for r in range(1, NZ):
        e2_copy(r).wait_send()
        e3_copy(r).wait_send()
    for i in range(3):
        e4_copy(i).wait_send()

    fr[me16] = fs[me16]
    frs[clip] = fss[clip]
    for par in range(2):
        @pl.when(lax.rem(clip, 2) == par)
        def _():
            wm, ws = pl.ds(0, mwidth(par)), pl.ds(0, swidth(par))
            for q in range(16):
                @pl.when(me16 != q)
                def _():
                    rcopy(fs.at[q, :, wm], fr.at[q, :, wm], f_s.at[q], f_r.at[q], core_dev).wait_recv()
            acc = fr[0, :, wm].astype(F32)
            for q in range(1, 16):
                acc = acc + fr[q, :, wm].astype(F32)
            gw_ref[:, :mwidth(par)] = acc
            for j in range(CLIPS):
                @pl.when(clip != j)
                def _():
                    rcopy(fss.at[j, :, ws], frs.at[j, :, ws], f2_s.at[j], f2_r.at[j], core_dev).wait_recv()
            acc = frs[0, :, ws].astype(F32)
            for j in range(1, CLIPS):
                acc = acc + frs[j, :, ws].astype(F32)
            gw_ref[:, mwidth(par):] = acc
    pltpu.make_async_copy(gw_ref, gw_out, loc.at[5]).start()

    pltpu.make_async_copy(ge_ref, ge_out, loc.at[4]).wait()
    pltpu.make_async_copy(gw_ref, gw_out, loc.at[5]).wait()
    for j in range(CLIPS):
        bo_copy(j).wait()
    pltpu.make_async_copy(ga_ref, ga_out, loc.at[7]).wait()


def fused(step, rewards, lat, noi, vc, vu, ew, gate, vals, w, cot):
    anyspace = pl.BlockSpec(memory_space=pl.ANY)
    dma = pltpu.SemaphoreType.DMA
    scratch = [
        pltpu.SMEM((1,), jnp.int32),
        pltpu.SMEM((1,), F32),
        pltpu.VMEM((CH, TOK), F32),
        pltpu.VMEM((CH, TOK), F32),
        pltpu.VMEM((CH, TOK), BF16),
        pltpu.VMEM((CH, TOK), BF16),
        pltpu.VMEM((CH, D), BF16),
        pltpu.VMEM((1, D), F32),
        pltpu.VMEM((TOK, H), BF16),
        pltpu.VMEM((2 * TOK, D), BF16),
        pltpu.VMEM((HALF, 2 * TOK), BF16),
        pltpu.VMEM((2, HALF, TOK), BF16),
        pltpu.VMEM((CLIPS, H, SL), BF16),
        pltpu.VMEM((NC, HALF, ZW), F32),
        pltpu.VMEM((32, D), F32),
        pltpu.VMEM((4, NC, ZROWS, ZW), BF16),
        pltpu.VMEM((4, NC, ZROWS, ZW), BF16),
        pltpu.VMEM((3, NC, ZROWS, ZW), BF16),
        pltpu.VMEM((3, NC, ZROWS, ZW), BF16),
        pltpu.VMEM((16, ROWS, 2 * THIRD), BF16),
        pltpu.VMEM((16, ROWS, 2 * THIRD), BF16),
        pltpu.VMEM((CLIPS, ROWS, 2 * THIRD), BF16),
        pltpu.VMEM((CLIPS, ROWS, 2 * THIRD), BF16),
        pltpu.VMEM((4, NZ, 16, SL), BF16),
        pltpu.VMEM((16, D), BF16),
        pltpu.VMEM((16, D), BF16),
        pltpu.VMEM((NZ, 16, SL), BF16),
        pltpu.VMEM((NZ, 16, SL), BF16),
        pltpu.VMEM((NZ, ROWS, SW), BF16),
        pltpu.VMEM((NZ, ROWS, SW), BF16),
        pltpu.VMEM((4, ROWS, SW), BF16),
        pltpu.VMEM((4, ROWS, SW), BF16),
        pltpu.VMEM((3, ROWS, SW), BF16),
        pltpu.VMEM((3, ROWS, SW), BF16),
        pltpu.VMEM((CH, D), F32),
        pltpu.VMEM((CH, D), BF16),
        pltpu.VMEM((32, D), BF16),
        pltpu.VMEM((HALF, NC * ZW), F32),
        pltpu.VMEM((8, 128), F32),
        pltpu.VMEM((CLIPS, 8, 128), F32),
        pltpu.VMEM((CH, TOK), BF16),
        pltpu.VMEM((TOK, CH), BF16),
        pltpu.VMEM((TOK, D), BF16),
        pltpu.VMEM((1, D), F32),
        pltpu.VMEM((8, 128), F32),
        pltpu.VMEM((TOK, H), F32),
        pltpu.VMEM((TOK, D), BF16),
        pltpu.VMEM((TOK, H), BF16),
        pltpu.VMEM((ROWS, SL), F32),
        pltpu.VMEM((CH, D), F32),
        dma((16,)), dma((7,)), dma((8,)), dma((NC,)), dma((NC,)), dma, dma,
        dma((9,)), dma((5,)), dma((16,)), dma((16,)), dma((16,)),
        dma((NZ,)), dma((NZ,)), dma((4,)), dma((4,)), dma((3,)), dma((3,)),
        dma((4 * NC,)), dma((4 * NC,)), dma((3 * NC,)), dma((3 * NC,)),
        dma((16,)), dma((16,)), dma((8,)), dma((8,)), dma((8,)), dma, dma, dma, dma, dma((7,)), dma((8,)), dma((7,)), dma((8,)), dma((3,)), dma((4,)),
    ]
    return pl.pallas_call(
        kernel,
        name="fused_step",
        out_shape=(
            jax.ShapeDtypeStruct((TOK, D), BF16),
            jax.ShapeDtypeStruct((TOK, H), BF16),
            jax.ShapeDtypeStruct((ROWS, SL), F32),
            jax.ShapeDtypeStruct((CH, D), F32),
        ),
        in_specs=[anyspace] * 11,
        out_specs=(anyspace, anyspace, anyspace, anyspace),
        scratch_shapes=scratch,
        compiler_params=pltpu.CompilerParams(
            collective_id=0, has_side_effects=True, vmem_limit_bytes=58 * 2**20
        ),
    )(step, rewards, lat, noi, vc, vu, ew, gate, vals, w, cot)


def copy_kernel(bo, ga, gw, ge, bo_o, ga_o, gw_o, ge_o, v0, v1, v2, v3, ins, outs):
    loads, stores = [], []
    n = 0
    for src, mid, dst, parts in ((bo, v0, bo_o, 4), (ga, v1, ga_o, 2), (ge, v3, ge_o, 2), (gw, v2, gw_o, 1)):
        rows = src.shape[0] // parts
        for p in range(parts):
            at = pl.ds(p * rows, rows)
            loads.append(pltpu.make_async_copy(src.at[at], mid.at[at], ins.at[n]))
            stores.append(pltpu.make_async_copy(mid.at[at], dst.at[at], outs.at[n]))
            n += 1
    for c in loads:
        c.start()
    for a, b in zip(loads, stores):
        a.wait()
        b.start()
    for c in stores:
        c.wait()


def copied(*arrays):
    anyspace = pl.BlockSpec(memory_space=pl.ANY)
    return pl.pallas_call(
        copy_kernel,
        name="results",
        out_shape=tuple(jax.ShapeDtypeStruct(a.shape, a.dtype) for a in arrays),
        in_specs=[anyspace] * 4,
        out_specs=(anyspace,) * 4,
        scratch_shapes=[pltpu.VMEM(a.shape, a.dtype) for a in arrays]
        + [pltpu.SemaphoreType.DMA((9,)), pltpu.SemaphoreType.DMA((9,))],
        compiler_params=pltpu.CompilerParams(vmem_limit_bytes=60 * 2**20),
    )(*arrays)


def local(latent, sample_noise, vel_cond, vel_uncond, step_index, embed_w, gate_scale, attn_vals, out_w, cotangent, rewards):
    bo, ga, gw, ge = copied(*fused(
        step_index, rewards, latent[0], sample_noise[0], vel_cond[0], vel_uncond[0], embed_w,
        gate_scale, attn_vals[0], out_w, cotangent[0],
    ))
    return bo[None], ga[None], gw, ge[None]


def solution(mesh):
    in_specs = (
        P("clip", None, "seq"),
        P("clip", None, "seq"),
        P("clip", None, "seq"),
        P("clip", None, "seq"),
        P(),
        P(),
        P("clip", None),
        P("clip", "seq", None),
        P(None, "clip"),
        P("clip", "seq", None),
        P("clip"),
    )
    out_specs = (
        P("clip", "seq", None),
        P("clip", "seq", None),
        P("seq", "clip"),
        P("clip", None, None),
    )
    return jax.shard_map(local, mesh=mesh, in_specs=in_specs, out_specs=out_specs, check_vma=False)
```
